32 devices in a mesh: node: 8 (over z, x), local: 4 (over y, core).
Axes of the slice: x: 2, y: 2, z: 4, core: 2. Of those that a mesh axis runs over, the one named last changes fastest.
Arguments:
- tokens: bfloat16 [512, 7168], P(('node', 'local')), may hold values from -6 to 6
- out_grads: bfloat16 [512, 7168], P(('node', 'local')), may hold values from -0.59765625 to 0.59765625
- routes: int32 [512, 8], P(('node', 'local')), may hold values from 0 to 15, as said below
- gate_values: float32 [512, 8], P(('node', 'local')), may hold values from 0.1 to 1
- gate_weight: bfloat16 [32, 7168, 512], P(('node', 'local')), may hold values from -0.0625 to 0.0625
- up_weight: bfloat16 [32, 7168, 512], P(('node', 'local')), may hold values from -0.0625 to 0.0625
- down_weight: bfloat16 [32, 512, 7168], P(('node', 'local')), may hold values from -0.1875 to 0.1875
Outputs:
- input_grads: bfloat16 [512, 7168], P(('node', 'local'))
- gate_grads: float32 [512, 8], P(('node', 'local'))
The draws below stay inside these ranges and needn't reach their ends.
Inputs may be any that keep to these rules, and one draw needn't show every extreme that they name: `routes`: each row names 8 different experts, 2 from each of 4 different groups (group of e is e // 2). Among the 16 rows of one device, at most 13 rows use a given group and at most 13 rows name a given expert; in every draw some group and some expert reach these bounds from every device.
All inputs are finite; a program needn't handle non-finite values.
Results may differ from the reference program's by a relative error of at most 0.012.
Values may be sent and summed in bfloat16 or wider, within the bound.
A program may use at most 128 MiB of HBM per device.

```python
import math
import jax
import jax.numpy as jnp
from jax import lax

D = 7168
HID = 1024
HALF = 512
TOPK = 8
NODE_LIMIT = 4
PER_NODE = 2
TOK_DEV = 16
TOKENS = 512
EXP_NODE = 2
EXPERTS = 16
CAP_NODE = 13
CAP_EXP = 13
N_NODE = 8
N_LOCAL = 4


def draw_routes(key, part):
    key = jax.random.fold_in(key, 7)
    hot_key, dev_base = jax.random.split(key)
    favored_node_index = jax.random.randint(hot_key, (), 0, N_NODE)
    favored_local_expert = jax.random.randint(jax.random.fold_in(hot_key, 1), (), 0, EXP_NODE)
    node_ids = jnp.arange(N_NODE, dtype=jnp.int32)
    local_expert_index = jnp.arange(EXP_NODE, dtype=jnp.int32)

    def one_device(dev_key):
        node_key, local_key = jax.random.split(dev_key)
        node_noise = jax.random.randint(node_key, (TOK_DEV, N_NODE), 0, 4096)
        local_noise = jax.random.randint(local_key, (TOK_DEV, N_NODE, EXP_NODE), 0, 4096)

        def choose(counters, noise_pair):
            node_count, local_count = counters
            node_row, local_row = noise_pair
            node_score = node_row * N_NODE + node_ids + jnp.where(node_ids == favored_node_index, 1 << 24, 0)
            node_score = jnp.where(node_count < CAP_NODE, node_score, -1 - node_ids)
            _, selected_experts = lax.top_k(node_score, NODE_LIMIT)
            local_expert_affinity = local_row[selected_experts] * EXP_NODE + local_expert_index[None, :]
            favored_score_boost = (selected_experts[:, None] == favored_node_index) & (local_expert_index[None, :] == favored_local_expert)
            local_expert_affinity = local_expert_affinity + jnp.where(favored_score_boost, 1 << 24, 0)
            has_room = local_count[selected_experts] < CAP_EXP
            local_expert_affinity = jnp.where(has_room, local_expert_affinity, -1 - local_expert_index[None, :])
            _, pick_ids = lax.top_k(local_expert_affinity, PER_NODE)
            node_mark = (node_ids[None, :] == selected_experts[:, None]).astype(jnp.int32)
            local_mark = jnp.sum((local_expert_index[None, None, :] == pick_ids[:, :, None]).astype(jnp.int32), axis=1)
            node_count = node_count + jnp.sum(node_mark, axis=0)
            local_count = local_count + jnp.sum(node_mark[:, :, None] * local_mark[:, None, :], axis=0)
            expert_row = (selected_experts[:, None] * EXP_NODE + pick_ids).reshape(TOPK)
            return ((node_count, local_count), expert_row)
        zero_state = (jnp.zeros((N_NODE,), jnp.int32), jnp.zeros((N_NODE, EXP_NODE), jnp.int32))
        _, route_rows = lax.scan(choose, zero_state, (node_noise, local_noise))
        return route_rows
    dev_keys = jax.random.split(dev_base, TOKENS // TOK_DEV)
    return jax.vmap(one_device)(dev_keys).reshape(TOKENS, TOPK).astype(jnp.int32)


def block_levels(own_key, extent, shards, low, top_value):
    loudness = 1.0
    for axis_at, blocks in shards:
        draws = jax.random.uniform(jax.random.fold_in(jax.random.fold_in(own_key, 6), axis_at), (blocks,), jnp.float32, low / len(shards), top_value / len(shards))
        loudness = loudness * jnp.repeat(jnp.exp(draws), extent[axis_at] // blocks).reshape((-1,) + (1,) * (len(extent) - 1 - axis_at))
    return loudness


def noise(stream_key, dims, spread, bound, pieces=(), kind=jnp.bfloat16):
    values = jax.random.normal(stream_key, dims, jnp.float32) * spread
    if len(pieces) > 0:
        values = block_levels(stream_key, dims, pieces, -0.22, 0.18) * values
    return jnp.clip(values, min=-bound, max=bound).astype(kind)


def setup_inputs(seed: int = 0) -> dict:
    key_list = jax.random.split(jax.random.key(seed), 8)
    tokens = noise(key_list[0], (TOKENS, D), 1.0, 6.0, ((0, 32),))
    out_grads = noise(key_list[1], (TOKENS, D), 0.1, 0.59765625, ((0, 32),))
    routes = draw_routes(jax.random.fold_in(key_list[7], 71), 0)
    gate_values = jnp.clip(jnp.exp(math.log(1.0) - 2.3025851 * jax.random.uniform(key_list[3], (TOKENS, TOPK), jnp.float32) ** block_levels(key_list[3], (TOKENS, TOPK), ((0, 32),), -0.2, 0.2)), 0.1, 1.0)
    gate_weight = noise(key_list[4], (2 * EXPERTS, D, HALF), D ** -0.5, 0.0625, ((0, 32),))
    up_weight = noise(key_list[5], (2 * EXPERTS, D, HALF), D ** -0.5, 0.0625, ((0, 32),))
    down_weight = noise(key_list[6], (2 * EXPERTS, HALF, D), HID ** -0.5, 0.1875, ((0, 32),))
    return {"tokens": tokens, "out_grads": out_grads, "routes": routes, "gate_values": gate_values, "gate_weight": gate_weight, "up_weight": up_weight, "down_weight": down_weight}


def shard_terms(rows_x, rows_dy, w_gate, w_up, w_down):
    pre_gate = jnp.dot(rows_x, w_gate, preferred_element_type=jnp.float32)
    pre_up = jnp.dot(rows_x, w_up, preferred_element_type=jnp.float32)
    sigmoid_gate = jax.nn.sigmoid(pre_gate)
    activated = pre_gate * sigmoid_gate
    hidden = (activated * pre_up).astype(jnp.bfloat16)
    back_grad = lax.dot_general(rows_dy, w_down, (((1,), (1,)), ((), ())), preferred_element_type=jnp.float32)
    part_gate = jnp.sum(hidden.astype(jnp.float32) * back_grad, axis=1)
    d_gate = (back_grad * pre_up * sigmoid_gate * (1.0 + pre_gate * (1.0 - sigmoid_gate))).astype(jnp.bfloat16)
    d_up = (back_grad * activated).astype(jnp.bfloat16)
    part_dx = lax.dot_general(d_gate, w_gate, (((1,), (1,)), ((), ())), preferred_element_type=jnp.float32)
    part_dx = part_dx + lax.dot_general(d_up, w_up, (((1,), (1,)), ((), ())), preferred_element_type=jnp.float32)
    gate_high = part_gate.astype(jnp.bfloat16)
    gate_low = (part_gate - gate_high.astype(jnp.float32)).astype(jnp.bfloat16)
    return part_dx.astype(jnp.bfloat16), gate_high, gate_low


def reference(tokens, out_grads, routes, gate_values, gate_weight, up_weight, down_weight):
    capacity = N_NODE * N_LOCAL * CAP_EXP

    def one_shard(totals, shard_id):
        dx_sum, gate_sum = totals
        expert = shard_id // 2
        is_routed = routes == expert
        routed = jnp.any(is_routed, axis=1)
        row_index = jnp.nonzero(routed, size=capacity, fill_value=TOKENS)[0].astype(jnp.int32)
        rows_x = jnp.take(tokens, row_index, axis=0, mode="fill", fill_value=0)
        rows_dy = jnp.take(out_grads, row_index, axis=0, mode="fill", fill_value=0)
        w_gate = lax.dynamic_index_in_dim(gate_weight, shard_id, 0, keepdims=False)
        w_up = lax.dynamic_index_in_dim(up_weight, shard_id, 0, keepdims=False)
        w_down = lax.dynamic_index_in_dim(down_weight, shard_id, 0, keepdims=False)
        part_dx, gate_high, gate_low = shard_terms(rows_x, rows_dy, w_gate, w_up, w_down)
        carried = gate_high.astype(jnp.float32) + gate_low.astype(jnp.float32)
        token_gate = jnp.sum(jnp.where(is_routed, gate_values, 0.0), axis=1)
        row_gate = jnp.take(token_gate, row_index, axis=0, mode="fill", fill_value=0)
        dx_sum = dx_sum.at[row_index].add(part_dx.astype(jnp.float32) * row_gate[:, None], mode="drop")
        gate_term = jnp.zeros((TOKENS,), jnp.float32).at[row_index].add(carried, mode="drop")
        gate_sum = gate_sum + jnp.where(is_routed, gate_term[:, None], 0.0)
        return (dx_sum, gate_sum), None

    zero_state = (jnp.zeros((TOKENS, D), jnp.float32), jnp.zeros((TOKENS, TOPK), jnp.float32))
    (dx_sum, gate_sum), _ = lax.scan(one_shard, zero_state, jnp.arange(2 * EXPERTS, dtype=jnp.int32))
    return dx_sum.astype(jnp.bfloat16), gate_sum
```

```python
import jax
import jax.numpy as jnp
from jax import lax
from jax.sharding import PartitionSpec as P

NODE_LIMIT = 4
PER_NODE = 2


def shard_terms(rows_x, rows_dy, w_gate, w_up, w_down):
    pre_gate = jnp.dot(rows_x, w_gate, preferred_element_type=jnp.float32)
    pre_up = jnp.dot(rows_x, w_up, preferred_element_type=jnp.float32)
    sigmoid_gate = jax.nn.sigmoid(pre_gate)
    activated = pre_gate * sigmoid_gate
    hidden = (activated * pre_up).astype(jnp.bfloat16)
    back_grad = lax.dot_general(
        rows_dy, w_down, (((1,), (1,)), ((), ())), preferred_element_type=jnp.float32
    )
    part_gate = jnp.sum(hidden.astype(jnp.float32) * back_grad, axis=1)
    d_gate = (back_grad * pre_up * sigmoid_gate * (1.0 + pre_gate * (1.0 - sigmoid_gate))).astype(
        jnp.bfloat16
    )
    d_up = (back_grad * activated).astype(jnp.bfloat16)
    part_dx = lax.dot_general(
        d_gate, w_gate, (((1,), (1,)), ((), ())), preferred_element_type=jnp.float32
    )
    part_dx = part_dx + lax.dot_general(
        d_up, w_up, (((1,), (1,)), ((), ())), preferred_element_type=jnp.float32
    )
    gate_high = part_gate.astype(jnp.bfloat16)
    gate_low = (part_gate - gate_high.astype(jnp.float32)).astype(jnp.bfloat16)
    return (part_dx.astype(jnp.bfloat16), jnp.stack([gate_high, gate_low], axis=-1))


def finish_slots(
    backward_input_gradient, back_gate, position, gate_values, slots, width, row_count, pick_count
):
    flat_index = position.reshape(-1)
    picked = jnp.take(backward_input_gradient.reshape(slots, width), flat_index, axis=0).reshape(
        row_count, pick_count, 2, width
    )
    weighted = jnp.sum(picked.astype(jnp.float32) * gate_values[:, :, None, None], axis=(1, 2))
    gate_parts = jnp.take(back_gate.reshape(slots, 2), flat_index, axis=0).astype(jnp.float32)
    gate_grads = jnp.sum(gate_parts.reshape(row_count, pick_count, 4), axis=2)
    return (weighted.astype(jnp.bfloat16), gate_grads)


def on_device(tokens, out_grads, routes, gate_values, gate_weight, up_weight, down_weight):
    n_node = lax.axis_size("node")
    n_local = lax.axis_size("local")
    devices = n_node * n_local
    row_count = tokens.shape[0]
    pick_count = routes.shape[1]
    width = tokens.shape[1]
    exp_node = n_local // 2
    experts = devices // 2
    node_capacity_limit = min(
        row_count, NODE_LIMIT * (row_count - 1) // (n_node - NODE_LIMIT + 1) + 1
    )
    cap_exp = min(
        node_capacity_limit, PER_NODE * (node_capacity_limit - 1) // (exp_node - PER_NODE + 1) + 1
    )
    w_gate = gate_weight[0]
    w_up = up_weight[0]
    w_down = down_weight[0]
    token_ids = jnp.arange(row_count, dtype=jnp.int32)
    half_ids = jnp.arange(2, dtype=jnp.int32)
    pick_ids = jnp.arange(pick_count, dtype=jnp.int32)
    expert_hot = routes[:, :, None] == jnp.arange(experts, dtype=jnp.int32)[None, None, :]
    per_expert = jnp.any(expert_hot, axis=1).astype(jnp.int32)
    expert_before = jnp.cumsum(per_expert, axis=0) - per_expert
    rank_e = jnp.sum(jnp.where(expert_hot, expert_before[:, None, :], 0), axis=2)
    dest_dev = 2 * routes[:, :, None] + half_ids[None, None, :]
    slots = devices * cap_exp
    node_of = routes // exp_node
    node_hot = node_of[:, :, None] == jnp.arange(n_node, dtype=jnp.int32)[None, None, :]
    per_node = jnp.any(node_hot, axis=1).astype(jnp.int32)
    node_before = jnp.cumsum(per_node, axis=0) - per_node
    node_rank = jnp.sum(jnp.where(node_hot, node_before[:, None, :], 0), axis=2)
    slot_one = (node_of * node_capacity_limit + node_rank).reshape(-1)
    same_before = (node_of[:, :, None] == node_of[:, None, :]) & (
        pick_ids[None, None, :] < pick_ids[None, :, None]
    )
    pick_slot = jnp.sum(same_before.astype(jnp.int32), axis=2).reshape(-1)
    slot_code = (1 + routes % exp_node * cap_exp + rank_e).reshape(-1)
    rows_one = n_node * node_capacity_limit
    owner_ids = jnp.broadcast_to(token_ids[:, None], routes.shape).reshape(-1)
    source_one = (
        jnp.full((rows_one,), row_count, jnp.int32).at[slot_one].set(owner_ids, mode="drop")
    )
    slot_codes = (
        jnp.zeros((rows_one, PER_NODE), jnp.float32)
        .at[slot_one, pick_slot]
        .set(slot_code.astype(jnp.float32), mode="drop")
    )
    slot_codes = slot_codes.astype(jnp.bfloat16).reshape(n_node, node_capacity_limit, PER_NODE)
    send_x = jnp.take(tokens, source_one, axis=0, mode="fill", fill_value=0).reshape(
        n_node, node_capacity_limit, width
    )
    send_dy = jnp.take(out_grads, source_one, axis=0, mode="fill", fill_value=0).reshape(
        n_node, node_capacity_limit, width
    )
    mid_x, mid_dy, mid_payload = (
        lax.all_to_all(send_x, "node", split_axis=0, concat_axis=0, tiled=True),
        lax.all_to_all(send_dy, "node", split_axis=0, concat_axis=0, tiled=True),
        lax.all_to_all(slot_codes, "node", split_axis=0, concat_axis=0, tiled=True),
    )
    mid_payload = mid_payload.reshape(rows_one, -1)
    code_int = mid_payload.astype(jnp.int32)
    is_live = code_int > 0
    local_pick = (code_int - 1) // cap_exp
    slot_rank = (code_int - 1) % cap_exp
    anchor = jnp.arange(rows_one, dtype=jnp.int32) // node_capacity_limit
    dest_two = (
        (2 * local_pick[:, :, None] + half_ids[None, None, :]) * n_node + anchor[:, None, None]
    ) * cap_exp + slot_rank[:, :, None]
    dest_two = jnp.where(is_live[:, :, None], dest_two, slots)
    mid_ids = jnp.broadcast_to(
        jnp.arange(rows_one, dtype=jnp.int32)[:, None, None], dest_two.shape
    ).reshape(-1)
    source_two = (
        jnp.full((slots,), rows_one, jnp.int32).at[dest_two.reshape(-1)].set(mid_ids, mode="drop")
    )
    out_x = jnp.take(mid_x.reshape(rows_one, width), source_two, axis=0, mode="fill", fill_value=0)
    out_dy = jnp.take(
        mid_dy.reshape(rows_one, width), source_two, axis=0, mode="fill", fill_value=0
    )
    got_x, got_dy = (
        lax.all_to_all(
            out_x.reshape(n_local, n_node * cap_exp, width),
            "local",
            split_axis=0,
            concat_axis=0,
            tiled=True,
        ),
        lax.all_to_all(
            out_dy.reshape(n_local, n_node * cap_exp, width),
            "local",
            split_axis=0,
            concat_axis=0,
            tiled=True,
        ),
    )
    part_dx, gate_pair = shard_terms(
        got_x.reshape(slots, width), got_dy.reshape(slots, width), w_gate, w_up, w_down
    )
    backward_input_gradient, back_gate = (
        lax.all_to_all(
            lax.all_to_all(
                part_dx.reshape(n_local, n_node, cap_exp, width),
                "node",
                split_axis=1,
                concat_axis=1,
                tiled=True,
            ),
            "local",
            split_axis=0,
            concat_axis=0,
            tiled=True,
        ),
        lax.all_to_all(
            lax.all_to_all(
                gate_pair.reshape(n_local, n_node, cap_exp, 2),
                "node",
                split_axis=1,
                concat_axis=1,
                tiled=True,
            ),
            "local",
            split_axis=0,
            concat_axis=0,
            tiled=True,
        ),
    )
    position = (dest_dev % n_local * n_node + dest_dev // n_local) * cap_exp + rank_e[:, :, None]
    return finish_slots(
        backward_input_gradient,
        back_gate,
        position,
        gate_values,
        slots,
        width,
        row_count,
        pick_count,
    )


def on_device_dense(tokens, out_grads, routes, gate_values, gate_weight, up_weight, down_weight):
    axes = ("node", "local")
    q = lax.axis_index("node") * lax.axis_size("local") + lax.axis_index("local")
    picks = jnp.concatenate([routes.astype(jnp.float32), gate_values], axis=1)
    picks = lax.all_gather(picks, axes, axis=0, tiled=True)
    rows_x = lax.all_gather(tokens, axes, axis=0, tiled=True)
    rows_dy = lax.all_gather(out_grads, axes, axis=0, tiled=True)
    pick_count = routes.shape[1]
    hot = picks[:, :pick_count] == (q // 2).astype(jnp.float32)
    weight = jnp.sum(jnp.where(hot, picks[:, pick_count:], 0.0), axis=1)
    w_gate = gate_weight[0]
    w_up = up_weight[0]
    w_down = down_weight[0]
    pre_gate = jnp.dot(rows_x, w_gate, preferred_element_type=jnp.float32)
    pre_up = jnp.dot(rows_x, w_up, preferred_element_type=jnp.float32)
    sigmoid_gate = jax.nn.sigmoid(pre_gate)
    activated = pre_gate * sigmoid_gate
    hidden = (activated * pre_up).astype(jnp.bfloat16)
    back_grad = lax.dot_general(
        rows_dy, w_down, (((1,), (1,)), ((), ())), preferred_element_type=jnp.float32
    )
    part_gate = jnp.sum(hidden.astype(jnp.float32) * back_grad, axis=1)
    d_gate = back_grad * pre_up * sigmoid_gate * (1.0 + pre_gate * (1.0 - sigmoid_gate))
    d_up = back_grad * activated
    part_dx = lax.dot_general(
        d_gate.astype(jnp.bfloat16),
        w_gate,
        (((1,), (1,)), ((), ())),
        preferred_element_type=jnp.float32,
    )
    part_dx = part_dx + lax.dot_general(
        d_up.astype(jnp.bfloat16),
        w_up,
        (((1,), (1,)), ((), ())),
        preferred_element_type=jnp.float32,
    )
    part_dx = jnp.where(weight[:, None] > 0.0, part_dx * weight[:, None], 0.0)
    gate_terms = jnp.where(hot, part_gate[:, None], 0.0)
    input_grads = lax.psum_scatter(
        part_dx.astype(jnp.bfloat16), axes, scatter_dimension=0, tiled=True
    )
    gate_grads = lax.psum_scatter(gate_terms, axes, scatter_dimension=0, tiled=True)
    return input_grads, gate_grads


def solution(mesh):
    devices = mesh.shape["node"] * mesh.shape["local"]
    in_specs = (
        P(("node", "local"), None),
        P(("node", "local"), None),
        P(("node", "local"), None),
        P(("node", "local"), None),
        P(("node", "local"), None, None),
        P(("node", "local"), None, None),
        P(("node", "local"), None, None),
    )
    out_specs = (P(("node", "local"), None), P(("node", "local"), None))
    body = on_device_dense if devices <= 32 else on_device
    return jax.shard_map(
        body, mesh=mesh, in_specs=in_specs, out_specs=out_specs, check_vma=False
    )
```

```python
import jax
import jax.numpy as jnp
from jax import lax
from jax.experimental import pallas as pl
from jax.experimental.pallas import tpu as pltpu
from jax.sharding import PartitionSpec as P

NODE_LIMIT = 4
PER_NODE = 2
MESH = pl.DeviceIdType.MESH
NT = (((1,), (1,)), ((), ()))


def shard_terms(rows_x, rows_dy, w_gate, w_up, w_down):
    pre_gate = jnp.dot(rows_x, w_gate, preferred_element_type=jnp.float32)
    pre_up = jnp.dot(rows_x, w_up, preferred_element_type=jnp.float32)
    sigmoid_gate = jax.nn.sigmoid(pre_gate)
    activated = pre_gate * sigmoid_gate
    hidden = (activated * pre_up).astype(jnp.bfloat16)
    back_grad = lax.dot_general(
        rows_dy, w_down, (((1,), (1,)), ((), ())), preferred_element_type=jnp.float32
    )
    part_gate = jnp.sum(hidden.astype(jnp.float32) * back_grad, axis=1)
    d_gate = (back_grad * pre_up * sigmoid_gate * (1.0 + pre_gate * (1.0 - sigmoid_gate))).astype(
        jnp.bfloat16
    )
    d_up = (back_grad * activated).astype(jnp.bfloat16)
    part_dx = lax.dot_general(
        d_gate, w_gate, (((1,), (1,)), ((), ())), preferred_element_type=jnp.float32
    )
    part_dx = part_dx + lax.dot_general(
        d_up, w_up, (((1,), (1,)), ((), ())), preferred_element_type=jnp.float32
    )
    gate_high = part_gate.astype(jnp.bfloat16)
    gate_low = (part_gate - gate_high.astype(jnp.float32)).astype(jnp.bfloat16)
    return (part_dx.astype(jnp.bfloat16), jnp.stack([gate_high, gate_low], axis=-1))


def finish_slots(
    backward_input_gradient, back_gate, position, gate_values, slots, width, row_count, pick_count
):
    flat_index = position.reshape(-1)
    picked = jnp.take(backward_input_gradient.reshape(slots, width), flat_index, axis=0).reshape(
        row_count, pick_count, 2, width
    )
    weighted = jnp.sum(picked.astype(jnp.float32) * gate_values[:, :, None, None], axis=(1, 2))
    gate_parts = jnp.take(back_gate.reshape(slots, 2), flat_index, axis=0).astype(jnp.float32)
    gate_grads = jnp.sum(gate_parts.reshape(row_count, pick_count, 4), axis=2)
    return (weighted.astype(jnp.bfloat16), gate_grads)


def on_device(tokens, out_grads, routes, gate_values, gate_weight, up_weight, down_weight):
    n_node = lax.axis_size("node")
    n_local = lax.axis_size("local")
    devices = n_node * n_local
    row_count = tokens.shape[0]
    pick_count = routes.shape[1]
    width = tokens.shape[1]
    exp_node = n_local // 2
    experts = devices // 2
    node_capacity_limit = min(
        row_count, NODE_LIMIT * (row_count - 1) // (n_node - NODE_LIMIT + 1) + 1
    )
    cap_exp = min(
        node_capacity_limit, PER_NODE * (node_capacity_limit - 1) // (exp_node - PER_NODE + 1) + 1
    )
    w_gate = gate_weight[0]
    w_up = up_weight[0]
    w_down = down_weight[0]
    token_ids = jnp.arange(row_count, dtype=jnp.int32)
    half_ids = jnp.arange(2, dtype=jnp.int32)
    pick_ids = jnp.arange(pick_count, dtype=jnp.int32)
    expert_hot = routes[:, :, None] == jnp.arange(experts, dtype=jnp.int32)[None, None, :]
    per_expert = jnp.any(expert_hot, axis=1).astype(jnp.int32)
    expert_before = jnp.cumsum(per_expert, axis=0) - per_expert
    rank_e = jnp.sum(jnp.where(expert_hot, expert_before[:, None, :], 0), axis=2)
    dest_dev = 2 * routes[:, :, None] + half_ids[None, None, :]
    slots = devices * cap_exp
    node_of = routes // exp_node
    node_hot = node_of[:, :, None] == jnp.arange(n_node, dtype=jnp.int32)[None, None, :]
    per_node = jnp.any(node_hot, axis=1).astype(jnp.int32)
    node_before = jnp.cumsum(per_node, axis=0) - per_node
    node_rank = jnp.sum(jnp.where(node_hot, node_before[:, None, :], 0), axis=2)
    slot_one = (node_of * node_capacity_limit + node_rank).reshape(-1)
    same_before = (node_of[:, :, None] == node_of[:, None, :]) & (
        pick_ids[None, None, :] < pick_ids[None, :, None]
    )
    pick_slot = jnp.sum(same_before.astype(jnp.int32), axis=2).reshape(-1)
    slot_code = (1 + routes % exp_node * cap_exp + rank_e).reshape(-1)
    rows_one = n_node * node_capacity_limit
    owner_ids = jnp.broadcast_to(token_ids[:, None], routes.shape).reshape(-1)
    source_one = (
        jnp.full((rows_one,), row_count, jnp.int32).at[slot_one].set(owner_ids, mode="drop")
    )
    slot_codes = (
        jnp.zeros((rows_one, PER_NODE), jnp.float32)
        .at[slot_one, pick_slot]
        .set(slot_code.astype(jnp.float32), mode="drop")
    )
    slot_codes = slot_codes.astype(jnp.bfloat16).reshape(n_node, node_capacity_limit, PER_NODE)
    send_x = jnp.take(tokens, source_one, axis=0, mode="fill", fill_value=0).reshape(
        n_node, node_capacity_limit, width
    )
    send_dy = jnp.take(out_grads, source_one, axis=0, mode="fill", fill_value=0).reshape(
        n_node, node_capacity_limit, width
    )
    mid_x, mid_dy, mid_payload = (
        lax.all_to_all(send_x, "node", split_axis=0, concat_axis=0, tiled=True),
        lax.all_to_all(send_dy, "node", split_axis=0, concat_axis=0, tiled=True),
        lax.all_to_all(slot_codes, "node", split_axis=0, concat_axis=0, tiled=True),
    )
    mid_payload = mid_payload.reshape(rows_one, -1)
    code_int = mid_payload.astype(jnp.int32)
    is_live = code_int > 0
    local_pick = (code_int - 1) // cap_exp
    slot_rank = (code_int - 1) % cap_exp
    anchor = jnp.arange(rows_one, dtype=jnp.int32) // node_capacity_limit
    dest_two = (
        (2 * local_pick[:, :, None] + half_ids[None, None, :]) * n_node + anchor[:, None, None]
    ) * cap_exp + slot_rank[:, :, None]
    dest_two = jnp.where(is_live[:, :, None], dest_two, slots)
    mid_ids = jnp.broadcast_to(
        jnp.arange(rows_one, dtype=jnp.int32)[:, None, None], dest_two.shape
    ).reshape(-1)
    source_two = (
        jnp.full((slots,), rows_one, jnp.int32).at[dest_two.reshape(-1)].set(mid_ids, mode="drop")
    )
    out_x = jnp.take(mid_x.reshape(rows_one, width), source_two, axis=0, mode="fill", fill_value=0)
    out_dy = jnp.take(
        mid_dy.reshape(rows_one, width), source_two, axis=0, mode="fill", fill_value=0
    )
    got_x, got_dy = (
        lax.all_to_all(
            out_x.reshape(n_local, n_node * cap_exp, width),
            "local",
            split_axis=0,
            concat_axis=0,
            tiled=True,
        ),
        lax.all_to_all(
            out_dy.reshape(n_local, n_node * cap_exp, width),
            "local",
            split_axis=0,
            concat_axis=0,
            tiled=True,
        ),
    )
    part_dx, gate_pair = shard_terms(
        got_x.reshape(slots, width), got_dy.reshape(slots, width), w_gate, w_up, w_down
    )
    backward_input_gradient, back_gate = (
        lax.all_to_all(
            lax.all_to_all(
                part_dx.reshape(n_local, n_node, cap_exp, width),
                "node",
                split_axis=1,
                concat_axis=1,
                tiled=True,
            ),
            "local",
            split_axis=0,
            concat_axis=0,
            tiled=True,
        ),
        lax.all_to_all(
            lax.all_to_all(
                gate_pair.reshape(n_local, n_node, cap_exp, 2),
                "node",
                split_axis=1,
                concat_axis=1,
                tiled=True,
            ),
            "local",
            split_axis=0,
            concat_axis=0,
            tiled=True,
        ),
    )
    position = (dest_dev % n_local * n_node + dest_dev // n_local) * cap_exp + rank_e[:, :, None]
    return finish_slots(
        backward_input_gradient,
        back_gate,
        position,
        gate_values,
        slots,
        width,
        row_count,
        pick_count,
    )


def pair_kernel(
    tok, dyo, aux, wg_hbm, wu_hbm, wd_hbm, dx_out, gate_out,
    gx, gdy, wg, wu, wd, pg, pu, bg, dg, du, part, from_sib, from_one, from_two, from_z,
    local_sem, ag_send, ag_recv, rs_send, rs_recv,
):
    width = tok.shape[1]
    node = lax.axis_index("node")
    local = lax.axis_index("local")
    z, x = node // 2, node % 2
    y, core = local // 2, local % 2
    sib = (node, y * 2 + (1 - core))
    x_nbr = (z * 2 + (1 - x), local)
    y_nbr = (node, (1 - y) * 2 + core)
    z_peer = [None] + [(((z + k) % 4) * 2 + x, local) for k in (1, 2, 3)]
    expert = (node * 4 + local) // 2

    weight_copies = [
        pltpu.make_async_copy(src, dst, local_sem.at[i])
        for i, (src, dst) in enumerate(((wg_hbm, wg), (wu_hbm, wu), (wd_hbm, wd)))
    ]
    own_copies = [
        pltpu.make_async_copy(tok, gx.at[pl.ds(0, 16), pl.ds(0, width)], local_sem.at[3]),
        pltpu.make_async_copy(aux, gx.at[pl.ds(0, 16), pl.ds(width, 128)], local_sem.at[4]),
        pltpu.make_async_copy(dyo, gdy.at[pl.ds(0, 16), :], local_sem.at[5]),
    ]
    for c in own_copies:
        c.start()

    barrier = pltpu.get_barrier_semaphore()
    for dev in [sib, x_nbr, y_nbr] + z_peer[1:]:
        pl.semaphore_signal(barrier, inc=1, device_id=dev, device_id_type=MESH)
    pl.semaphore_wait(barrier, 6)
    for c in own_copies:
        c.wait()

    buffers = (gx, gdy)
    first_nbr = (x_nbr, y_nbr)
    second_nbr = (y_nbr, x_nbr)
    sends = []
    counts = [0, 0]

    def slot(second, dc, first, r):
        return second * 16 + dc * 8 + first * 4 + r

    def block(a, s):
        return buffers[a].at[pl.ds(s * 16, 16), :]

    def push(a, src, dst, dev):
        c = pltpu.make_async_remote_copy(
            src_ref=block(a, src),
            dst_ref=block(a, dst),
            send_sem=ag_send.at[a, counts[a]],
            recv_sem=ag_recv.at[a, dst],
            device_id=dev,
            device_id_type=MESH,
        )
        counts[a] += 1
        c.start()
        sends.append(c)

    def arrived(a, s):
        pltpu.make_async_remote_copy(
            src_ref=block(a, s),
            dst_ref=block(a, s),
            send_sem=ag_send.at[a, 0],
            recv_sem=ag_recv.at[a, s],
            device_id=sib,
            device_id_type=MESH,
        ).wait_recv()

    def spread(a, second, first, r):
        src = slot(second, 0, first, r)
        if second == 0 and first == 0:
            push(a, src, slot(0, 0, 1, r), first_nbr[a])
        if second == 0:
            push(a, src, slot(1, 0, first, r), second_nbr[a])
        push(a, src, slot(second, 1, first, r), sib)

    for k in (1, 2, 3):
        for a in (0, 1):
            push(a, 0, slot(0, 0, 0, 4 - k), z_peer[k])
    for a in (0, 1):
        spread(a, 0, 0, 0)
    for c in weight_copies:
        c.start()
    order = (0, 1, 3, 2)
    for r in order[1:]:
        for a in (0, 1):
            arrived(a, slot(0, 0, 0, r))
            spread(a, 0, 0, r)
    for r in order:
        for a in (0, 1):
            arrived(a, slot(0, 0, 1, r))
            spread(a, 0, 1, r)

    step = 1792

    def forward(half):
        rows = pl.ds(half * 256, 256)
        for acc, w in ((pg, wg), (pu, wu)):
            acc[rows, :] = jnp.zeros((256, 512), jnp.float32)

        def body(k, carry):
            cols = pl.ds(pl.multiple_of(k * step, 256), step)
            left = gx[rows, cols]
            pg[rows, :] += jnp.dot(left, wg[cols, :], preferred_element_type=jnp.float32)
            pu[rows, :] += jnp.dot(left, wu[cols, :], preferred_element_type=jnp.float32)
            return carry

        lax.fori_loop(0, width // step, body, 0)

    def backward(half):
        rows = pl.ds(half * 256, 256)
        bg[rows, :] = jnp.zeros((256, 512), jnp.float32)

        def body(k, carry):
            cols = pl.ds(pl.multiple_of(k * step, 256), step)
            bg[rows, :] += lax.dot_general(
                gdy[rows, cols], wd[:, cols], NT, preferred_element_type=jnp.float32
            )
            return carry

        lax.fori_loop(0, width // step, body, 0)

    for c in weight_copies:
        c.wait()
    for a in (0, 1):
        for first in (0, 1):
            for r in order:
                arrived(a, slot(0, 1, first, r))
        (forward, backward)[a](0)
    for first in (0, 1):
        for r in order:
            for a in (0, 1):
                arrived(a, slot(1, 0, first, r))
                spread(a, 1, first, r)
    for a in (0, 1):
        for first in (0, 1):
            for r in order:
                arrived(a, slot(1, 1, first, r))
        (forward, backward)[a](1)

    lane = lax.broadcasted_iota(jnp.int32, (64, 128), 1)
    for dc in (1, 0):
        for dy in (0, 1):
            for dx in (0, 1):
                at_x = pl.ds((dy * 4 + dc * 2 + dx) * 64, 64)
                at_dy = pl.ds((dx * 4 + dc * 2 + dy) * 64, 64)
                group = dc * 4 + dy * 2 + dx
                at = pl.ds(group * 64, 64)
                info = gx[at_x, pl.ds(width, 128)].astype(jnp.float32)
                hot = (lane % 16 == expert) & (lane < 48)
                weight = jnp.sum(jnp.where(hot, info, 0.0), axis=1, keepdims=True)
                pick = jnp.sum(
                    jnp.where(lane == 48 + expert, info, 0.0), axis=1, keepdims=True
                )
                pre_gate = pg[at_x, :]
                pre_up = pu[at_x, :]
                back = bg[at_dy, :]
                sig = jax.nn.sigmoid(pre_gate)
                act = pre_gate * sig
                hidden = (act * pre_up).astype(jnp.bfloat16).astype(jnp.float32)
                part_gate = jnp.sum(hidden * back, axis=1, keepdims=True)
                dg[at, :] = (
                    weight * (back * pre_up * sig * (1.0 + pre_gate * (1.0 - sig)))
                ).astype(jnp.bfloat16)
                du[at, :] = (weight * (back * act)).astype(jnp.bfloat16)
                term = jnp.where(
                    (lane + 1).astype(jnp.float32) == pick, jnp.broadcast_to(part_gate, (64, 128)), 0.0
                )
                high = term.astype(jnp.bfloat16)
                low = (term - high.astype(jnp.float32)).astype(jnp.bfloat16)
                blocks = pl.ds(group * 4, 4)
                part[blocks, :, pl.ds(width, 128)] = high.reshape(4, 16, 128)
                part[blocks, :, pl.ds(width + 128, 128)] = low.reshape(4, 16, 128)

    quarter = width // 4
    pieces = [pl.ds(p * quarter, quarter + (256 if p == 3 else 0)) for p in range(4)]

    def product(dc, p):
        rows = pl.ds(dc * 256, 256)

        def body(n, carry):
            cols = pl.ds(pl.multiple_of(p * quarter + n * 256, 256), 256)
            out = lax.dot_general(
                dg[rows, :], wg[cols, :], NT, preferred_element_type=jnp.float32
            ) + lax.dot_general(du[rows, :], wu[cols, :], NT, preferred_element_type=jnp.float32)
            part[pl.ds(dc * 16, 16), :, cols] = out.astype(jnp.bfloat16).reshape(16, 16, 256)
            return carry

        lax.fori_loop(0, quarter // 256, body, 0)

    def rs_copy(p, lane_at, src, dst, dev):
        return pltpu.make_async_remote_copy(
            src_ref=src,
            dst_ref=dst,
            send_sem=rs_send.at[p, lane_at],
            recv_sem=rs_recv.at[p, lane_at],
            device_id=dev,
            device_id_type=MESH,
        )

    def add(base, got, got_base, n, cols):
        def body(i, carry):
            total = part[base + i, :, cols].astype(jnp.float32) + got[
                got_base + i, :, cols
            ].astype(jnp.float32)
            part[base + i, :, cols] = total.astype(jnp.bfloat16)
            return carry

        lax.fori_loop(0, n, body, 0)

    flight = {}

    def launch(p, name, *copies):
        for c in copies:
            c.start()
            sends.append(c)
        flight[p, name] = copies

    def landed(p, name):
        for c in flight[p, name]:
            c.wait_recv()

    def stage_sib(p):
        cols = pieces[p]
        launch(p, 0, rs_copy(p, 0, part.at[pl.ds(16, 16), :, cols], from_sib.at[:, :, cols], sib))

    def stage_one(p):
        cols = pieces[p]
        landed(p, 0)
        add(0, from_sib, 0, 16, pl.ds(p * quarter, quarter))
        if p == 3:
            hi, lo = pl.ds(width, 128), pl.ds(width + 128, 128)

            def body(i, carry):
                total = (
                    part[i, :, hi].astype(jnp.float32)
                    + part[i, :, lo].astype(jnp.float32)
                    + from_sib[i, :, hi].astype(jnp.float32)
                    + from_sib[i, :, lo].astype(jnp.float32)
                )
                high = total.astype(jnp.bfloat16)
                part[i, :, hi] = high
                part[i, :, lo] = (total - high.astype(jnp.float32)).astype(jnp.bfloat16)
                return carry

            lax.fori_loop(0, 16, body, 0)
        if p % 2 == 0:
            launch(p, 1, rs_copy(p, 1, part.at[pl.ds(8, 8), :, cols], from_one.at[:, :, cols], y_nbr))
        else:
            launch(
                p,
                1,
                rs_copy(p, 1, part.at[pl.ds(4, 4), :, cols], from_one.at[pl.ds(0, 4), :, cols], x_nbr),
                rs_copy(p, 2, part.at[pl.ds(12, 4), :, cols], from_one.at[pl.ds(4, 4), :, cols], x_nbr),
            )

    def stage_two(p):
        cols = pieces[p]
        landed(p, 1)
        if p % 2 == 0:
            add(0, from_one, 0, 8, cols)
            launch(p, 2, rs_copy(p, 3, part.at[pl.ds(4, 4), :, cols], from_two.at[:, :, cols], x_nbr))
        else:
            add(0, from_one, 0, 4, cols)
            add(8, from_one, 4, 4, cols)
            launch(p, 2, rs_copy(p, 3, part.at[pl.ds(8, 4), :, cols], from_two.at[:, :, cols], y_nbr))

    def stage_three(p):
        cols = pieces[p]
        landed(p, 2)
        add(0, from_two, 0, 4, cols)
        launch(
            p,
            3,
            *[
                rs_copy(p, 3 + r, part.at[r, :, cols], from_z.at[r - 1, :, cols], z_peer[r])
                for r in (2, 1, 3)
            ],
        )

    def stage_last(p):
        landed(p, 3)

        def total(cols):
            return (
                part[0, :, cols].astype(jnp.float32)
                + from_z[0, :, cols].astype(jnp.float32)
                + from_z[1, :, cols].astype(jnp.float32)
                + from_z[2, :, cols].astype(jnp.float32)
            )

        cols = pl.ds(p * quarter, quarter)
        dx_out[:, cols] = total(cols).astype(jnp.bfloat16)
        if p == 3:
            gate_out[...] = total(pl.ds(width, 128)) + total(pl.ds(width + 128, 128))

    for p in range(4):
        product(1, p)
        stage_sib(p)
        product(0, p)
        stage_one(p)
    for pair in ((0, 1), (2, 3)):
        for stage in (stage_two, stage_three):
            for p in pair:
                stage(p)
    for p in range(4):
        stage_last(p)
    for c in sends:
        c.wait_send()


def on_device_kernel(tokens, out_grads, routes, gate_values, gate_weight, up_weight, down_weight):
    rows, width = tokens.shape
    experts = lax.axis_size("node") * lax.axis_size("local") // 2
    hot = routes[:, :, None] == jnp.arange(experts, dtype=jnp.int32)[None, None, :]
    table = jnp.sum(jnp.where(hot, gate_values[:, :, None], 0.0), axis=1)
    high = lax.reduce_precision(table, 8, 7)
    mid = lax.reduce_precision(table - high, 8, 7)
    low = table - high - mid
    picks = jnp.arange(1, routes.shape[1] + 1, dtype=jnp.float32)[None, :, None]
    pick = jnp.sum(jnp.where(hot, picks, 0.0), axis=1)
    aux = jnp.concatenate([high, mid, low, pick], axis=1)
    aux = jnp.pad(aux, ((0, 0), (0, 128 - 4 * experts))).astype(jnp.bfloat16)
    half = gate_weight.shape[2]
    total = width + 256
    bf16, f32 = jnp.bfloat16, jnp.float32
    dx, gate = pl.pallas_call(
        pair_kernel,
        out_shape=(
            jax.ShapeDtypeStruct((rows, width), bf16),
            jax.ShapeDtypeStruct((rows, 128), f32),
        ),
        in_specs=[pl.BlockSpec(memory_space=pl.ANY)] * 6,
        out_specs=(
            pl.BlockSpec(memory_space=pltpu.VMEM),
            pl.BlockSpec(memory_space=pltpu.VMEM),
        ),
        scratch_shapes=[
            pltpu.VMEM((512, width + 128), bf16),
            pltpu.VMEM((512, width), bf16),
            pltpu.VMEM((width, half), bf16),
            pltpu.VMEM((width, half), bf16),
            pltpu.VMEM((half, width), bf16),
            pltpu.VMEM((512, half), f32),
            pltpu.VMEM((512, half), f32),
            pltpu.VMEM((512, half), f32),
            pltpu.VMEM((512, half), bf16),
            pltpu.VMEM((512, half), bf16),
            pltpu.VMEM((32, 16, total), bf16),
            pltpu.VMEM((16, 16, total), bf16),
            pltpu.VMEM((8, 16, total), bf16),
            pltpu.VMEM((4, 16, total), bf16),
            pltpu.VMEM((3, 16, total), bf16),
            pltpu.SemaphoreType.DMA((6,)),
            pltpu.SemaphoreType.DMA((2, 32)),
            pltpu.SemaphoreType.DMA((2, 32)),
            pltpu.SemaphoreType.DMA((4, 8)),
            pltpu.SemaphoreType.DMA((4, 8)),
        ],
        compiler_params=pltpu.CompilerParams(
            collective_id=0, has_side_effects=True, vmem_limit_bytes=62 * 1024 * 1024
        ),
        cost_estimate=pl.CostEstimate(
            flops=10 * 512 * width * half, bytes_accessed=6 * width * half, transcendentals=0
        ),
    )(tokens, out_grads, aux, gate_weight[0], up_weight[0], down_weight[0])
    return dx, gate[:, : routes.shape[1]]


def solution(mesh):
    small = mesh.shape["node"] == 8 and mesh.shape["local"] == 4
    in_specs = (
        P(("node", "local"), None),
        P(("node", "local"), None),
        P(("node", "local"), None),
        P(("node", "local"), None),
        P(("node", "local"), None, None),
        P(("node", "local"), None, None),
        P(("node", "local"), None, None),
    )
    out_specs = (P(("node", "local"), None), P(("node", "local"), None))
    body = on_device_kernel if small else on_device
    return jax.shard_map(
        body, mesh=mesh, in_specs=in_specs, out_specs=out_specs, check_vma=False
    )
```

```python
import jax
import jax.numpy as jnp
from jax import lax
from jax.experimental import pallas as pl
from jax.experimental.pallas import tpu as pltpu
from jax.sharding import PartitionSpec as P

NODE_LIMIT = 4
PER_NODE = 2
MESH = pl.DeviceIdType.MESH
NT = (((1,), (1,)), ((), ()))


def shard_terms(rows_x, rows_dy, w_gate, w_up, w_down):
    pre_gate = jnp.dot(rows_x, w_gate, preferred_element_type=jnp.float32)
    pre_up = jnp.dot(rows_x, w_up, preferred_element_type=jnp.float32)
    sigmoid_gate = jax.nn.sigmoid(pre_gate)
    activated = pre_gate * sigmoid_gate
    hidden = (activated * pre_up).astype(jnp.bfloat16)
    back_grad = lax.dot_general(
        rows_dy, w_down, (((1,), (1,)), ((), ())), preferred_element_type=jnp.float32
    )
    part_gate = jnp.sum(hidden.astype(jnp.float32) * back_grad, axis=1)
    d_gate = (back_grad * pre_up * sigmoid_gate * (1.0 + pre_gate * (1.0 - sigmoid_gate))).astype(
        jnp.bfloat16
    )
    d_up = (back_grad * activated).astype(jnp.bfloat16)
    part_dx = lax.dot_general(
        d_gate, w_gate, (((1,), (1,)), ((), ())), preferred_element_type=jnp.float32
    )
    part_dx = part_dx + lax.dot_general(
        d_up, w_up, (((1,), (1,)), ((), ())), preferred_element_type=jnp.float32
    )
    gate_high = part_gate.astype(jnp.bfloat16)
    gate_low = (part_gate - gate_high.astype(jnp.float32)).astype(jnp.bfloat16)
    return (part_dx.astype(jnp.bfloat16), jnp.stack([gate_high, gate_low], axis=-1))


def finish_slots(
    backward_input_gradient, back_gate, position, gate_values, slots, width, row_count, pick_count
):
    flat_index = position.reshape(-1)
    picked = jnp.take(backward_input_gradient.reshape(slots, width), flat_index, axis=0).reshape(
        row_count, pick_count, 2, width
    )
    weighted = jnp.sum(picked.astype(jnp.float32) * gate_values[:, :, None, None], axis=(1, 2))
    gate_parts = jnp.take(back_gate.reshape(slots, 2), flat_index, axis=0).astype(jnp.float32)
    gate_grads = jnp.sum(gate_parts.reshape(row_count, pick_count, 4), axis=2)
    return (weighted.astype(jnp.bfloat16), gate_grads)


def on_device(tokens, out_grads, routes, gate_values, gate_weight, up_weight, down_weight):
    n_node = lax.axis_size("node")
    n_local = lax.axis_size("local")
    devices = n_node * n_local
    row_count = tokens.shape[0]
    pick_count = routes.shape[1]
    width = tokens.shape[1]
    exp_node = n_local // 2
    experts = devices // 2
    node_capacity_limit = min(
        row_count, NODE_LIMIT * (row_count - 1) // (n_node - NODE_LIMIT + 1) + 1
    )
    cap_exp = min(
        node_capacity_limit, PER_NODE * (node_capacity_limit - 1) // (exp_node - PER_NODE + 1) + 1
    )
    w_gate = gate_weight[0]
    w_up = up_weight[0]
    w_down = down_weight[0]
    token_ids = jnp.arange(row_count, dtype=jnp.int32)
    half_ids = jnp.arange(2, dtype=jnp.int32)
    pick_ids = jnp.arange(pick_count, dtype=jnp.int32)
    expert_hot = routes[:, :, None] == jnp.arange(experts, dtype=jnp.int32)[None, None, :]
    per_expert = jnp.any(expert_hot, axis=1).astype(jnp.int32)
    expert_before = jnp.cumsum(per_expert, axis=0) - per_expert
    rank_e = jnp.sum(jnp.where(expert_hot, expert_before[:, None, :], 0), axis=2)
    dest_dev = 2 * routes[:, :, None] + half_ids[None, None, :]
    slots = devices * cap_exp
    node_of = routes // exp_node
    node_hot = node_of[:, :, None] == jnp.arange(n_node, dtype=jnp.int32)[None, None, :]
    per_node = jnp.any(node_hot, axis=1).astype(jnp.int32)
    node_before = jnp.cumsum(per_node, axis=0) - per_node
    node_rank = jnp.sum(jnp.where(node_hot, node_before[:, None, :], 0), axis=2)
    slot_one = (node_of * node_capacity_limit + node_rank).reshape(-1)
    same_before = (node_of[:, :, None] == node_of[:, None, :]) & (
        pick_ids[None, None, :] < pick_ids[None, :, None]
    )
    pick_slot = jnp.sum(same_before.astype(jnp.int32), axis=2).reshape(-1)
    slot_code = (1 + routes % exp_node * cap_exp + rank_e).reshape(-1)
    rows_one = n_node * node_capacity_limit
    owner_ids = jnp.broadcast_to(token_ids[:, None], routes.shape).reshape(-1)
    source_one = (
        jnp.full((rows_one,), row_count, jnp.int32).at[slot_one].set(owner_ids, mode="drop")
    )
    slot_codes = (
        jnp.zeros((rows_one, PER_NODE), jnp.float32)
        .at[slot_one, pick_slot]
        .set(slot_code.astype(jnp.float32), mode="drop")
    )
    slot_codes = slot_codes.astype(jnp.bfloat16).reshape(n_node, node_capacity_limit, PER_NODE)
    send_x = jnp.take(tokens, source_one, axis=0, mode="fill", fill_value=0).reshape(
        n_node, node_capacity_limit, width
    )
    send_dy = jnp.take(out_grads, source_one, axis=0, mode="fill", fill_value=0).reshape(
        n_node, node_capacity_limit, width
    )
    mid_x, mid_dy, mid_payload = (
        lax.all_to_all(send_x, "node", split_axis=0, concat_axis=0, tiled=True),
        lax.all_to_all(send_dy, "node", split_axis=0, concat_axis=0, tiled=True),
        lax.all_to_all(slot_codes, "node", split_axis=0, concat_axis=0, tiled=True),
    )
    mid_payload = mid_payload.reshape(rows_one, -1)
    code_int = mid_payload.astype(jnp.int32)
    is_live = code_int > 0
    local_pick = (code_int - 1) // cap_exp
    slot_rank = (code_int - 1) % cap_exp
    anchor = jnp.arange(rows_one, dtype=jnp.int32) // node_capacity_limit
    dest_two = (
        (2 * local_pick[:, :, None] + half_ids[None, None, :]) * n_node + anchor[:, None, None]
    ) * cap_exp + slot_rank[:, :, None]
    dest_two = jnp.where(is_live[:, :, None], dest_two, slots)
    mid_ids = jnp.broadcast_to(
        jnp.arange(rows_one, dtype=jnp.int32)[:, None, None], dest_two.shape
    ).reshape(-1)
    source_two = (
        jnp.full((slots,), rows_one, jnp.int32).at[dest_two.reshape(-1)].set(mid_ids, mode="drop")
    )
    out_x = jnp.take(mid_x.reshape(rows_one, width), source_two, axis=0, mode="fill", fill_value=0)
    out_dy = jnp.take(
        mid_dy.reshape(rows_one, width), source_two, axis=0, mode="fill", fill_value=0
    )
    got_x, got_dy = (
        lax.all_to_all(
            out_x.reshape(n_local, n_node * cap_exp, width),
            "local",
            split_axis=0,
            concat_axis=0,
            tiled=True,
        ),
        lax.all_to_all(
            out_dy.reshape(n_local, n_node * cap_exp, width),
            "local",
            split_axis=0,
            concat_axis=0,
            tiled=True,
        ),
    )
    part_dx, gate_pair = shard_terms(
        got_x.reshape(slots, width), got_dy.reshape(slots, width), w_gate, w_up, w_down
    )
    backward_input_gradient, back_gate = (
        lax.all_to_all(
            lax.all_to_all(
                part_dx.reshape(n_local, n_node, cap_exp, width),
                "node",
                split_axis=1,
                concat_axis=1,
                tiled=True,
            ),
            "local",
            split_axis=0,
            concat_axis=0,
            tiled=True,
        ),
        lax.all_to_all(
            lax.all_to_all(
                gate_pair.reshape(n_local, n_node, cap_exp, 2),
                "node",
                split_axis=1,
                concat_axis=1,
                tiled=True,
            ),
            "local",
            split_axis=0,
            concat_axis=0,
            tiled=True,
        ),
    )
    position = (dest_dev % n_local * n_node + dest_dev // n_local) * cap_exp + rank_e[:, :, None]
    return finish_slots(
        backward_input_gradient,
        back_gate,
        position,
        gate_values,
        slots,
        width,
        row_count,
        pick_count,
    )


def pair_kernel(
    tok, dyo, aux, wg_hbm, wu_hbm, wd_hbm, dx_out, gate_out,
    gx, gdy, wg, wu, wd, pg, pu, bg, dg, du, part, from_sib, from_one, from_two, from_z,
    local_sem, ag_send, ag_recv, rs_send, rs_recv,
):
    width = tok.shape[1]
    node = lax.axis_index("node")
    local = lax.axis_index("local")
    z, x = node // 2, node % 2
    y, core = local // 2, local % 2
    sib = (node, y * 2 + (1 - core))
    x_nbr = (z * 2 + (1 - x), local)
    y_nbr = (node, (1 - y) * 2 + core)
    z_peer = [None] + [(((z + k) % 4) * 2 + x, local) for k in (1, 2, 3)]
    expert = (node * 4 + local) // 2

    weight_copies = [
        pltpu.make_async_copy(src, dst, local_sem.at[i])
        for i, (src, dst) in enumerate(((wg_hbm, wg), (wu_hbm, wu), (wd_hbm, wd)))
    ]
    own_copies = [
        pltpu.make_async_copy(tok, gx.at[pl.ds(0, 16), pl.ds(0, width)], local_sem.at[3]),
        pltpu.make_async_copy(aux, gx.at[pl.ds(0, 16), pl.ds(width, 128)], local_sem.at[4]),
        pltpu.make_async_copy(dyo, gdy.at[pl.ds(0, 16), :], local_sem.at[5]),
    ]
    for c in own_copies:
        c.start()

    barrier = pltpu.get_barrier_semaphore()
    for dev in [sib, x_nbr, y_nbr] + z_peer[1:]:
        pl.semaphore_signal(barrier, inc=1, device_id=dev, device_id_type=MESH)
    pl.semaphore_wait(barrier, 6)
    for c in own_copies:
        c.wait()

    buffers = (gx, gdy)
    first_nbr = (x_nbr, y_nbr)
    second_nbr = (y_nbr, x_nbr)
    early = 1024
    sends = []
    counts = [0, 0, 0, 0]

    def slot(second, dc, first, r):
        return second * 16 + dc * 8 + first * 4 + r

    def block(a, e, s):
        whole = buffers[a].shape[1]
        cols = pl.ds(0, early) if e == 0 else pl.ds(early, whole - early)
        return buffers[a].at[pl.ds(pl.multiple_of(s * 16, 16), 16), cols]

    def push(a, e, src, dst, dev, cond=None):
        kind = a * 2 + e
        c = pltpu.make_async_remote_copy(
            src_ref=block(a, e, src),
            dst_ref=block(a, e, dst),
            send_sem=ag_send.at[kind, counts[kind]],
            recv_sem=ag_recv.at[kind, dst],
            device_id=dev,
            device_id_type=MESH,
        )
        counts[kind] += 1
        if cond is None:
            c.start()
        else:
            pl.when(cond)(c.start)
        sends.append((cond, c))

    def arrived(a, e, s):
        pltpu.make_async_remote_copy(
            src_ref=block(a, e, s),
            dst_ref=block(a, e, s),
            send_sem=ag_send.at[a * 2 + e, 0],
            recv_sem=ag_recv.at[a * 2 + e, s],
            device_id=sib,
            device_id_type=MESH,
        ).wait_recv()

    def chain_own(a, e, second, first):
        base = slot(second, 0, first, 0)
        push(a, e, base, base + 3, (node + 2, local), z < 3)
        push(a, e, base, base + 1, (node - 2, local), z > 0)

    def chain(a, e, second, first, r):
        base = slot(second, 0, first, 0)
        up = z + r >= 4
        target = jnp.where(up, node + 2, node - 2)
        onward = (up & (z < 3)) | (jnp.logical_not(up) & (z > 0))
        push(a, e, base + r, base + jnp.where(up, r - 1, r + 1), (target, local), onward)

    def to_first(a, e, second, first, r):
        push(a, e, slot(second, 0, first, r), slot(second, 0, 1, r), first_nbr[a])

    def to_second(a, e, second, first, r):
        push(a, e, slot(second, 0, first, r), slot(1, 0, first, r), second_nbr[a])

    def to_sib(a, e, second, first, r):
        push(a, e, slot(second, 0, first, r), slot(second, 1, first, r), sib)

    middle = (z == 1) | (z == 2)
    far = (
        jnp.where(z == 3, 3, 1),
        jnp.where(middle, 3, 2),
        jnp.where(middle, 2, jnp.where(z == 0, 3, 1)),
    )
    both = (0, 1)

    for a in both:
        chain_own(a, 1, 0, 0)
    for a in both:
        to_first(a, 0, 0, 0, 0)
    for a in both:
        to_second(a, 0, 0, 0, 0)
    for a in both:
        to_first(a, 1, 0, 0, 0)
    for a in both:
        to_second(a, 1, 0, 0, 0)
    for a in both:
        chain_own(a, 0, 0, 0)
    for a in both:
        to_sib(a, 1, 0, 0, 0)
        to_sib(a, 0, 0, 0, 0)
    for c in weight_copies:
        c.start()
    for a in both:
        arrived(a, 0, slot(0, 0, 1, 0))
        to_second(a, 0, 0, 1, 0)

    def z_main(j):
        for a in both:
            arrived(a, 1, slot(0, 0, 0, far[j]))
            chain(a, 1, 0, 0, far[j])
            to_first(a, 1, 0, 0, far[j])
            to_second(a, 1, 0, 0, far[j])
            to_sib(a, 1, 0, 0, far[j])

    def first_main(r):
        for a in both:
            arrived(a, 1, slot(0, 0, 1, r))
            to_second(a, 1, 0, 1, r)
            to_sib(a, 1, 0, 1, r)

    def z_early(j):
        for second, first in ((0, 0), (0, 1), (1, 0), (1, 1)):
            for a in both:
                arrived(a, 0, slot(second, 0, first, far[j]))
                chain(a, 0, second, first, far[j])
                to_sib(a, 0, second, first, far[j])

    def second_main(first, r):
        for a in both:
            arrived(a, 1, slot(1, 0, first, r))
            to_sib(a, 1, 1, first, r)

    z_main(0)
    for a in both:
        chain_own(a, 0, 0, 1)
        to_sib(a, 0, 0, 1, 0)
    for first in (0, 1):
        for a in both:
            arrived(a, 0, slot(1, 0, first, 0))
            chain_own(a, 0, 1, first)
            to_sib(a, 0, 1, first, 0)
    z_main(1)
    first_main(0)
    z_main(2)
    z_early(0)
    first_main(far[0])
    z_early(1)
    first_main(far[1])
    first_main(far[2])

    step = 1536

    def forward(row, n, start, tiles, width_k):
        rows = pl.ds(row, n)

        def body(k, carry):
            cols = pl.ds(pl.multiple_of(start + k * width_k, 256), width_k)
            left = gx[rows, cols]
            pg[rows, :] += jnp.dot(left, wg[cols, :], preferred_element_type=jnp.float32)
            pu[rows, :] += jnp.dot(left, wu[cols, :], preferred_element_type=jnp.float32)
            return carry

        lax.fori_loop(0, tiles, body, 0)

    def backward(row, n, start, tiles, width_k):
        rows = pl.ds(row, n)

        def body(k, carry):
            cols = pl.ds(pl.multiple_of(start + k * width_k, 256), width_k)
            bg[rows, :] += lax.dot_general(
                gdy[rows, cols], wd[:, cols], NT, preferred_element_type=jnp.float32
            )
            return carry

        lax.fori_loop(0, tiles, body, 0)

    def clear(i, carry):
        rows = pl.ds(pl.multiple_of(i * 64, 64), 64)
        for acc in (pg, pu, bg):
            acc[rows, :] = jnp.zeros((64, 512), jnp.float32)
        return carry

    lax.fori_loop(0, 8, clear, 0)
    for c in weight_copies:
        c.wait()
    main_tiles = (width - early) // step
    for a in both:
        for first in (0, 1):
            for r in range(4):
                arrived(a, 1, slot(0, 1, first, r))
        (forward, backward)[a](0, 256, early, main_tiles, step)
        if a == 0:
            z_early(2)
    for r in (0,) + far:
        second_main(0, r)
    for r in (0,) + far:
        second_main(1, r)
    for a in both:
        for second in (0, 1):
            for first in (0, 1):
                for r in range(4):
                    arrived(a, 0, slot(second, 1, first, r))
        (forward, backward)[a](0, 512, 0, 2, early // 2)
    for a in both:
        for first in (0, 1):
            for r in range(4):
                arrived(a, 1, slot(1, 1, first, r))
        (forward, backward)[a](256, 256, early, main_tiles, step)

    lane = lax.broadcasted_iota(jnp.int32, (64, 128), 1)
    for dc in (1, 0):
        for dy in (0, 1):
            for dx in (0, 1):
                at_x = pl.ds((dy * 4 + dc * 2 + dx) * 64, 64)
                at_dy = pl.ds((dx * 4 + dc * 2 + dy) * 64, 64)
                group = dc * 4 + dy * 2 + dx
                at = pl.ds(group * 64, 64)
                info = gx[at_x, pl.ds(width, 128)].astype(jnp.float32)
                hot = (lane % 16 == expert) & (lane < 48)
                weight = jnp.sum(jnp.where(hot, info, 0.0), axis=1, keepdims=True)
                pick = jnp.sum(
                    jnp.where(lane == 48 + expert, info, 0.0), axis=1, keepdims=True
                )
                pre_gate = pg[at_x, :]
                pre_up = pu[at_x, :]
                back = bg[at_dy, :]
                sig = jax.nn.sigmoid(pre_gate)
                act = pre_gate * sig
                hidden = (act * pre_up).astype(jnp.bfloat16).astype(jnp.float32)
                part_gate = jnp.sum(hidden * back, axis=1, keepdims=True)
                dg[at, :] = (
                    weight * (back * pre_up * sig * (1.0 + pre_gate * (1.0 - sig)))
                ).astype(jnp.bfloat16)
                du[at, :] = (weight * (back * act)).astype(jnp.bfloat16)
                term = jnp.where(
                    (lane + 1).astype(jnp.float32) == pick, jnp.broadcast_to(part_gate, (64, 128)), 0.0
                )
                high = term.astype(jnp.bfloat16)
                low = (term - high.astype(jnp.float32)).astype(jnp.bfloat16)
                blocks = pl.ds(group * 4, 4)
                part[blocks, :, pl.ds(width, 128)] = high.reshape(4, 16, 128)
                part[blocks, :, pl.ds(width + 128, 128)] = low.reshape(4, 16, 128)

    quarter = width // 4
    pieces = [pl.ds(p * quarter, quarter + (256 if p == 3 else 0)) for p in range(4)]

    def product(dc, p):
        rows = pl.ds(dc * 256, 256)

        def body(n, carry):
            cols = pl.ds(pl.multiple_of(p * quarter + n * 256, 256), 256)
            out = lax.dot_general(
                dg[rows, :], wg[cols, :], NT, preferred_element_type=jnp.float32
            ) + lax.dot_general(du[rows, :], wu[cols, :], NT, preferred_element_type=jnp.float32)
            part[pl.ds(dc * 16, 16), :, cols] = out.astype(jnp.bfloat16).reshape(16, 16, 256)
            return carry

        lax.fori_loop(0, quarter // 256, body, 0)

    def rs_copy(p, lane_at, src, dst, dev):
        return pltpu.make_async_remote_copy(
            src_ref=src,
            dst_ref=dst,
            send_sem=rs_send.at[p, lane_at],
            recv_sem=rs_recv.at[p, lane_at],
            device_id=dev,
            device_id_type=MESH,
        )

    def add(base, got, got_base, n, cols):
        def body(i, carry):
            total = part[base + i, :, cols].astype(jnp.float32) + got[
                got_base + i, :, cols
            ].astype(jnp.float32)
            part[base + i, :, cols] = total.astype(jnp.bfloat16)
            return carry

        lax.fori_loop(0, n, body, 0)

    flight = {}

    def launch(p, name, *copies):
        for c in copies:
            c.start()
            sends.append((None, c))
        flight[p, name] = copies

    def landed(p, name):
        for c in flight[p, name]:
            c.wait_recv()

    def stage_sib(p):
        cols = pieces[p]
        launch(p, 0, rs_copy(p, 0, part.at[pl.ds(16, 16), :, cols], from_sib.at[:, :, cols], sib))

    def stage_one(p):
        cols = pieces[p]
        landed(p, 0)
        add(0, from_sib, 0, 16, pl.ds(p * quarter, quarter))
        if p == 3:
            hi, lo = pl.ds(width, 128), pl.ds(width + 128, 128)

            def body(i, carry):
                total = (
                    part[i, :, hi].astype(jnp.float32)
                    + part[i, :, lo].astype(jnp.float32)
                    + from_sib[i, :, hi].astype(jnp.float32)
                    + from_sib[i, :, lo].astype(jnp.float32)
                )
                high = total.astype(jnp.bfloat16)
                part[i, :, hi] = high
                part[i, :, lo] = (total - high.astype(jnp.float32)).astype(jnp.bfloat16)
                return carry

            lax.fori_loop(0, 16, body, 0)
        if p % 2 == 0:
            launch(p, 1, rs_copy(p, 1, part.at[pl.ds(8, 8), :, cols], from_one.at[:, :, cols], y_nbr))
        else:
            launch(
                p,
                1,
                rs_copy(p, 1, part.at[pl.ds(4, 4), :, cols], from_one.at[pl.ds(0, 4), :, cols], x_nbr),
                rs_copy(p, 2, part.at[pl.ds(12, 4), :, cols], from_one.at[pl.ds(4, 4), :, cols], x_nbr),
            )

    def stage_two(p):
        cols = pieces[p]
        landed(p, 1)
        if p % 2 == 0:
            add(0, from_one, 0, 8, cols)
            launch(p, 2, rs_copy(p, 3, part.at[pl.ds(4, 4), :, cols], from_two.at[:, :, cols], x_nbr))
        else:
            add(0, from_one, 0, 4, cols)
            add(8, from_one, 4, 4, cols)
            launch(p, 2, rs_copy(p, 3, part.at[pl.ds(8, 4), :, cols], from_two.at[:, :, cols], y_nbr))

    def stage_three(p):
        cols = pieces[p]
        landed(p, 2)
        add(0, from_two, 0, 4, cols)
        launch(
            p,
            3,
            *[
                rs_copy(p, 3 + r, part.at[r, :, cols], from_z.at[r - 1, :, cols], z_peer[r])
                for r in (2, 1, 3)
            ],
        )

    def stage_last(p):
        landed(p, 3)

        def total(cols):
            return (
                part[0, :, cols].astype(jnp.float32)
                + from_z[0, :, cols].astype(jnp.float32)
                + from_z[1, :, cols].astype(jnp.float32)
                + from_z[2, :, cols].astype(jnp.float32)
            )

        cols = pl.ds(p * quarter, quarter)
        dx_out[:, cols] = total(cols).astype(jnp.bfloat16)
        if p == 3:
            gate_out[...] = total(pl.ds(width, 128)) + total(pl.ds(width + 128, 128))

    for p in range(4):
        product(1, p)
        stage_sib(p)
        product(0, p)
        stage_one(p)
    for pair in ((0, 1), (2, 3)):
        for stage in (stage_two, stage_three):
            for p in pair:
                stage(p)
    for p in range(4):
        stage_last(p)
    for cond, c in sends:
        if cond is None:
            c.wait_send()
        else:
            pl.when(cond)(c.wait_send)


def on_device_kernel(tokens, out_grads, routes, gate_values, gate_weight, up_weight, down_weight):
    rows, width = tokens.shape
    experts = lax.axis_size("node") * lax.axis_size("local") // 2
    hot = routes[:, :, None] == jnp.arange(experts, dtype=jnp.int32)[None, None, :]
    table = jnp.sum(jnp.where(hot, gate_values[:, :, None], 0.0), axis=1)
    high = lax.reduce_precision(table, 8, 7)
    mid = lax.reduce_precision(table - high, 8, 7)
    low = table - high - mid
    picks = jnp.arange(1, routes.shape[1] + 1, dtype=jnp.float32)[None, :, None]
    pick = jnp.sum(jnp.where(hot, picks, 0.0), axis=1)
    aux = jnp.concatenate([high, mid, low, pick], axis=1)
    aux = jnp.pad(aux, ((0, 0), (0, 128 - 4 * experts))).astype(jnp.bfloat16)
    half = gate_weight.shape[2]
    total = width + 256
    bf16, f32 = jnp.bfloat16, jnp.float32
    dx, gate = pl.pallas_call(
        pair_kernel,
        out_shape=(
            jax.ShapeDtypeStruct((rows, width), bf16),
            jax.ShapeDtypeStruct((rows, 128), f32),
        ),
        in_specs=[pl.BlockSpec(memory_space=pl.ANY)] * 6,
        out_specs=(
            pl.BlockSpec(memory_space=pltpu.VMEM),
            pl.BlockSpec(memory_space=pltpu.VMEM),
        ),
        scratch_shapes=[
            pltpu.VMEM((512, width + 128), bf16),
            pltpu.VMEM((512, width), bf16),
            pltpu.VMEM((width, half), bf16),
            pltpu.VMEM((width, half), bf16),
            pltpu.VMEM((half, width), bf16),
            pltpu.VMEM((512, half), f32),
            pltpu.VMEM((512, half), f32),
            pltpu.VMEM((512, half), f32),
            pltpu.VMEM((512, half), bf16),
            pltpu.VMEM((512, half), bf16),
            pltpu.VMEM((32, 16, total), bf16),
            pltpu.VMEM((16, 16, total), bf16),
            pltpu.VMEM((8, 16, total), bf16),
            pltpu.VMEM((4, 16, total), bf16),
            pltpu.VMEM((3, 16, total), bf16),
            pltpu.SemaphoreType.DMA((6,)),
            pltpu.SemaphoreType.DMA((4, 40)),
            pltpu.SemaphoreType.DMA((4, 32)),
            pltpu.SemaphoreType.DMA((4, 8)),
            pltpu.SemaphoreType.DMA((4, 8)),
        ],
        compiler_params=pltpu.CompilerParams(
            collective_id=0, has_side_effects=True, vmem_limit_bytes=62 * 1024 * 1024
        ),
        cost_estimate=pl.CostEstimate(
            flops=10 * 512 * width * half, bytes_accessed=6 * width * half, transcendentals=0
        ),
    )(tokens, out_grads, aux, gate_weight[0], up_weight[0], down_weight[0])
    return dx, gate[:, : routes.shape[1]]


def solution(mesh):
    small = mesh.shape["node"] == 8 and mesh.shape["local"] == 4
    in_specs = (
        P(("node", "local"), None),
        P(("node", "local"), None),
        P(("node", "local"), None),
        P(("node", "local"), None),
        P(("node", "local"), None, None),
        P(("node", "local"), None, None),
        P(("node", "local"), None, None),
    )
    out_specs = (P(("node", "local"), None), P(("node", "local"), None))
    body = on_device_kernel if small else on_device
    return jax.shard_map(
        body, mesh=mesh, in_specs=in_specs, out_specs=out_specs, check_vma=False
    )
```

```python
import jax
import jax.numpy as jnp
from jax import lax
from jax.experimental import pallas as pl
from jax.experimental.pallas import tpu as pltpu
from jax.sharding import PartitionSpec as P

NODE_LIMIT = 4
PER_NODE = 2
MESH = pl.DeviceIdType.MESH
NT = (((1,), (1,)), ((), ()))


def shard_terms(rows_x, rows_dy, w_gate, w_up, w_down):
    pre_gate = jnp.dot(rows_x, w_gate, preferred_element_type=jnp.float32)
    pre_up = jnp.dot(rows_x, w_up, preferred_element_type=jnp.float32)
    sigmoid_gate = jax.nn.sigmoid(pre_gate)
    activated = pre_gate * sigmoid_gate
    hidden = (activated * pre_up).astype(jnp.bfloat16)
    back_grad = lax.dot_general(
        rows_dy, w_down, (((1,), (1,)), ((), ())), preferred_element_type=jnp.float32
    )
    part_gate = jnp.sum(hidden.astype(jnp.float32) * back_grad, axis=1)
    d_gate = (back_grad * pre_up * sigmoid_gate * (1.0 + pre_gate * (1.0 - sigmoid_gate))).astype(
        jnp.bfloat16
    )
    d_up = (back_grad * activated).astype(jnp.bfloat16)
    part_dx = lax.dot_general(
        d_gate, w_gate, (((1,), (1,)), ((), ())), preferred_element_type=jnp.float32
    )
    part_dx = part_dx + lax.dot_general(
        d_up, w_up, (((1,), (1,)), ((), ())), preferred_element_type=jnp.float32
    )
    gate_high = part_gate.astype(jnp.bfloat16)
    gate_low = (part_gate - gate_high.astype(jnp.float32)).astype(jnp.bfloat16)
    return (part_dx.astype(jnp.bfloat16), jnp.stack([gate_high, gate_low], axis=-1))


def finish_slots(
    backward_input_gradient, back_gate, position, gate_values, slots, width, row_count, pick_count
):
    flat_index = position.reshape(-1)
    picked = jnp.take(backward_input_gradient.reshape(slots, width), flat_index, axis=0).reshape(
        row_count, pick_count, 2, width
    )
    weighted = jnp.sum(picked.astype(jnp.float32) * gate_values[:, :, None, None], axis=(1, 2))
    gate_parts = jnp.take(back_gate.reshape(slots, 2), flat_index, axis=0).astype(jnp.float32)
    gate_grads = jnp.sum(gate_parts.reshape(row_count, pick_count, 4), axis=2)
    return (weighted.astype(jnp.bfloat16), gate_grads)


def on_device(tokens, out_grads, routes, gate_values, gate_weight, up_weight, down_weight):
    n_node = lax.axis_size("node")
    n_local = lax.axis_size("local")
    devices = n_node * n_local
    row_count = tokens.shape[0]
    pick_count = routes.shape[1]
    width = tokens.shape[1]
    exp_node = n_local // 2
    experts = devices // 2
    node_capacity_limit = min(
        row_count, NODE_LIMIT * (row_count - 1) // (n_node - NODE_LIMIT + 1) + 1
    )
    cap_exp = min(
        node_capacity_limit, PER_NODE * (node_capacity_limit - 1) // (exp_node - PER_NODE + 1) + 1
    )
    w_gate = gate_weight[0]
    w_up = up_weight[0]
    w_down = down_weight[0]
    token_ids = jnp.arange(row_count, dtype=jnp.int32)
    half_ids = jnp.arange(2, dtype=jnp.int32)
    pick_ids = jnp.arange(pick_count, dtype=jnp.int32)
    expert_hot = routes[:, :, None] == jnp.arange(experts, dtype=jnp.int32)[None, None, :]
    per_expert = jnp.any(expert_hot, axis=1).astype(jnp.int32)
    expert_before = jnp.cumsum(per_expert, axis=0) - per_expert
    rank_e = jnp.sum(jnp.where(expert_hot, expert_before[:, None, :], 0), axis=2)
    dest_dev = 2 * routes[:, :, None] + half_ids[None, None, :]
    slots = devices * cap_exp
    node_of = routes // exp_node
    node_hot = node_of[:, :, None] == jnp.arange(n_node, dtype=jnp.int32)[None, None, :]
    per_node = jnp.any(node_hot, axis=1).astype(jnp.int32)
    node_before = jnp.cumsum(per_node, axis=0) - per_node
    node_rank = jnp.sum(jnp.where(node_hot, node_before[:, None, :], 0), axis=2)
    slot_one = (node_of * node_capacity_limit + node_rank).reshape(-1)
    same_before = (node_of[:, :, None] == node_of[:, None, :]) & (
        pick_ids[None, None, :] < pick_ids[None, :, None]
    )
    pick_slot = jnp.sum(same_before.astype(jnp.int32), axis=2).reshape(-1)
    slot_code = (1 + routes % exp_node * cap_exp + rank_e).reshape(-1)
    rows_one = n_node * node_capacity_limit
    owner_ids = jnp.broadcast_to(token_ids[:, None], routes.shape).reshape(-1)
    source_one = (
        jnp.full((rows_one,), row_count, jnp.int32).at[slot_one].set(owner_ids, mode="drop")
    )
    slot_codes = (
        jnp.zeros((rows_one, PER_NODE), jnp.float32)
        .at[slot_one, pick_slot]
        .set(slot_code.astype(jnp.float32), mode="drop")
    )
    slot_codes = slot_codes.astype(jnp.bfloat16).reshape(n_node, node_capacity_limit, PER_NODE)
    send_x = jnp.take(tokens, source_one, axis=0, mode="fill", fill_value=0).reshape(
        n_node, node_capacity_limit, width
    )
    send_dy = jnp.take(out_grads, source_one, axis=0, mode="fill", fill_value=0).reshape(
        n_node, node_capacity_limit, width
    )
    mid_x, mid_dy, mid_payload = (
        lax.all_to_all(send_x, "node", split_axis=0, concat_axis=0, tiled=True),
        lax.all_to_all(send_dy, "node", split_axis=0, concat_axis=0, tiled=True),
        lax.all_to_all(slot_codes, "node", split_axis=0, concat_axis=0, tiled=True),
    )
    mid_payload = mid_payload.reshape(rows_one, -1)
    code_int = mid_payload.astype(jnp.int32)
    is_live = code_int > 0
    local_pick = (code_int - 1) // cap_exp
    slot_rank = (code_int - 1) % cap_exp
    anchor = jnp.arange(rows_one, dtype=jnp.int32) // node_capacity_limit
    dest_two = (
        (2 * local_pick[:, :, None] + half_ids[None, None, :]) * n_node + anchor[:, None, None]
    ) * cap_exp + slot_rank[:, :, None]
    dest_two = jnp.where(is_live[:, :, None], dest_two, slots)
    mid_ids = jnp.broadcast_to(
        jnp.arange(rows_one, dtype=jnp.int32)[:, None, None], dest_two.shape
    ).reshape(-1)
    source_two = (
        jnp.full((slots,), rows_one, jnp.int32).at[dest_two.reshape(-1)].set(mid_ids, mode="drop")
    )
    out_x = jnp.take(mid_x.reshape(rows_one, width), source_two, axis=0, mode="fill", fill_value=0)
    out_dy = jnp.take(
        mid_dy.reshape(rows_one, width), source_two, axis=0, mode="fill", fill_value=0
    )
    got_x, got_dy = (
        lax.all_to_all(
            out_x.reshape(n_local, n_node * cap_exp, width),
            "local",
            split_axis=0,
            concat_axis=0,
            tiled=True,
        ),
        lax.all_to_all(
            out_dy.reshape(n_local, n_node * cap_exp, width),
            "local",
            split_axis=0,
            concat_axis=0,
            tiled=True,
        ),
    )
    part_dx, gate_pair = shard_terms(
        got_x.reshape(slots, width), got_dy.reshape(slots, width), w_gate, w_up, w_down
    )
    backward_input_gradient, back_gate = (
        lax.all_to_all(
            lax.all_to_all(
                part_dx.reshape(n_local, n_node, cap_exp, width),
                "node",
                split_axis=1,
                concat_axis=1,
                tiled=True,
            ),
            "local",
            split_axis=0,
            concat_axis=0,
            tiled=True,
        ),
        lax.all_to_all(
            lax.all_to_all(
                gate_pair.reshape(n_local, n_node, cap_exp, 2),
                "node",
                split_axis=1,
                concat_axis=1,
                tiled=True,
            ),
            "local",
            split_axis=0,
            concat_axis=0,
            tiled=True,
        ),
    )
    position = (dest_dev % n_local * n_node + dest_dev // n_local) * cap_exp + rank_e[:, :, None]
    return finish_slots(
        backward_input_gradient,
        back_gate,
        position,
        gate_values,
        slots,
        width,
        row_count,
        pick_count,
    )


def pair_kernel(
    tok, dyo, aux, wg_hbm, wu_hbm, wd_hbm, dx_out, gate_out,
    gx, gdy, wg, wu, wd, pg, pu, bg, dg, du, part, from_sib, from_one, from_two, from_z,
    local_sem, ag_send, ag_recv, rs_send, rs_recv,
):
    width = tok.shape[1]
    node = lax.axis_index("node")
    local = lax.axis_index("local")
    z, x = node // 2, node % 2
    y, core = local // 2, local % 2
    sib = (node, y * 2 + (1 - core))
    x_nbr = (z * 2 + (1 - x), local)
    y_nbr = (node, (1 - y) * 2 + core)
    z_peer = [None] + [(((z + k) % 4) * 2 + x, local) for k in (1, 2, 3)]
    expert = (node * 4 + local) // 2

    weight_copies = [
        pltpu.make_async_copy(src, dst, local_sem.at[i])
        for i, (src, dst) in enumerate(((wg_hbm, wg), (wu_hbm, wu), (wd_hbm, wd)))
    ]
    own_copies = [
        pltpu.make_async_copy(tok, gx.at[pl.ds(0, 16), pl.ds(0, width)], local_sem.at[3]),
        pltpu.make_async_copy(aux, gx.at[pl.ds(0, 16), pl.ds(width, 128)], local_sem.at[4]),
        pltpu.make_async_copy(dyo, gdy.at[pl.ds(0, 16), :], local_sem.at[5]),
    ]
    for c in own_copies:
        c.start()

    barrier = pltpu.get_barrier_semaphore()
    for dev in [sib, x_nbr, y_nbr] + z_peer[1:]:
        pl.semaphore_signal(barrier, inc=1, device_id=dev, device_id_type=MESH)
    pl.semaphore_wait(barrier, 6)
    for c in own_copies:
        c.wait()

    buffers = (gx, gdy)
    first_nbr = (x_nbr, y_nbr)
    second_nbr = (y_nbr, x_nbr)
    early = 1024
    sends = []
    counts = [0, 0, 0, 0]

    def slot(second, dc, first, r):
        return second * 16 + dc * 8 + first * 4 + r

    def block(a, e, s):
        whole = buffers[a].shape[1]
        cols = pl.ds(0, early) if e == 0 else pl.ds(early, whole - early)
        return buffers[a].at[pl.ds(pl.multiple_of(s * 16, 16), 16), cols]

    def push(a, e, src, dst, dev, cond=None):
        kind = a * 2 + e
        c = pltpu.make_async_remote_copy(
            src_ref=block(a, e, src),
            dst_ref=block(a, e, dst),
            send_sem=ag_send.at[kind, counts[kind]],
            recv_sem=ag_recv.at[kind, dst],
            device_id=dev,
            device_id_type=MESH,
        )
        counts[kind] += 1
        if cond is None:
            c.start()
        else:
            pl.when(cond)(c.start)
        sends.append((cond, c))

    def arrived(a, e, s):
        pltpu.make_async_remote_copy(
            src_ref=block(a, e, s),
            dst_ref=block(a, e, s),
            send_sem=ag_send.at[a * 2 + e, 0],
            recv_sem=ag_recv.at[a * 2 + e, s],
            device_id=sib,
            device_id_type=MESH,
        ).wait_recv()

    def chain_own(a, e, second, first):
        base = slot(second, 0, first, 0)
        push(a, e, base, base + 3, (node + 2, local), z < 3)
        push(a, e, base, base + 1, (node - 2, local), z > 0)

    def chain(a, e, second, first, r):
        base = slot(second, 0, first, 0)
        up = z + r >= 4
        target = jnp.where(up, node + 2, node - 2)
        onward = (up & (z < 3)) | (jnp.logical_not(up) & (z > 0))
        push(a, e, base + r, base + jnp.where(up, r - 1, r + 1), (target, local), onward)

    def to_first(a, e, second, first, r):
        push(a, e, slot(second, 0, first, r), slot(second, 0, 1, r), first_nbr[a])

    def to_second(a, e, second, first, r):
        push(a, e, slot(second, 0, first, r), slot(1, 0, first, r), second_nbr[a])

    def to_sib(a, e, second, first, r):
        push(a, e, slot(second, 0, first, r), slot(second, 1, first, r), sib)

    middle = (z == 1) | (z == 2)
    far = (
        jnp.where(z == 3, 3, 1),
        jnp.where(middle, 3, 2),
        jnp.where(middle, 2, jnp.where(z == 0, 3, 1)),
    )
    both = (0, 1)

    for a in both:
        chain_own(a, 1, 0, 0)
    for a in both:
        to_first(a, 0, 0, 0, 0)
    for a in both:
        to_second(a, 0, 0, 0, 0)
    for a in both:
        to_first(a, 1, 0, 0, 0)
    for a in both:
        to_second(a, 1, 0, 0, 0)
    for a in both:
        chain_own(a, 0, 0, 0)
    for a in both:
        to_sib(a, 1, 0, 0, 0)
        to_sib(a, 0, 0, 0, 0)
    for c in weight_copies:
        c.start()
    for a in both:
        arrived(a, 0, slot(0, 0, 1, 0))
        to_second(a, 0, 0, 1, 0)

    def z_main(j):
        for a in both:
            arrived(a, 1, slot(0, 0, 0, far[j]))
            chain(a, 1, 0, 0, far[j])
            to_first(a, 1, 0, 0, far[j])
            to_second(a, 1, 0, 0, far[j])
            to_sib(a, 1, 0, 0, far[j])

    def first_main(r):
        for a in both:
            arrived(a, 1, slot(0, 0, 1, r))
            to_second(a, 1, 0, 1, r)
            to_sib(a, 1, 0, 1, r)

    def z_early(j):
        for second, first in ((0, 0), (0, 1), (1, 0), (1, 1)):
            for a in both:
                arrived(a, 0, slot(second, 0, first, far[j]))
                chain(a, 0, second, first, far[j])
                to_sib(a, 0, second, first, far[j])

    def second_main(first, r):
        for a in both:
            arrived(a, 1, slot(1, 0, first, r))
            to_sib(a, 1, 1, first, r)

    z_main(0)
    for a in both:
        chain_own(a, 0, 0, 1)
        to_sib(a, 0, 0, 1, 0)
    for first in (0, 1):
        for a in both:
            arrived(a, 0, slot(1, 0, first, 0))
            chain_own(a, 0, 1, first)
            to_sib(a, 0, 1, first, 0)
    z_main(1)
    first_main(0)
    z_main(2)
    z_early(0)
    first_main(far[0])
    z_early(1)
    first_main(far[1])
    first_main(far[2])

    step = 1536

    def forward(row, n, start, tiles, width_k):
        rows = pl.ds(row, n)

        def body(k, carry):
            cols = pl.ds(pl.multiple_of(start + k * width_k, 256), width_k)
            left = gx[rows, cols]
            pg[rows, :] += jnp.dot(left, wg[cols, :], preferred_element_type=jnp.float32)
            pu[rows, :] += jnp.dot(left, wu[cols, :], preferred_element_type=jnp.float32)
            return carry

        lax.fori_loop(0, tiles, body, 0)

    def backward(row, n, start, tiles, width_k):
        rows = pl.ds(row, n)

        def body(k, carry):
            cols = pl.ds(pl.multiple_of(start + k * width_k, 256), width_k)
            bg[rows, :] += lax.dot_general(
                gdy[rows, cols], wd[:, cols], NT, preferred_element_type=jnp.float32
            )
            return carry

        lax.fori_loop(0, tiles, body, 0)

    def clear(i, carry):
        rows = pl.ds(pl.multiple_of(i * 64, 64), 64)
        for acc in (pg, pu, bg):
            acc[rows, :] = jnp.zeros((64, 512), jnp.float32)
        return carry

    lax.fori_loop(0, 8, clear, 0)
    for c in weight_copies:
        c.wait()
    main_tiles = (width - early) // step
    for a in both:
        for first in (0, 1):
            for r in range(4):
                arrived(a, 1, slot(0, 1, first, r))
        (forward, backward)[a](0, 256, early, main_tiles, step)
        if a == 0:
            z_early(2)
    for r in (0,) + far:
        second_main(0, r)
    for a in both:
        for second in (0, 1):
            for first in (0, 1):
                for r in range(4):
                    arrived(a, 0, slot(second, 1, first, r))
        (forward, backward)[a](0, 512, 0, 2, early // 2)
    for r in (0,) + far:
        second_main(1, r)
    for a in both:
        for first in (0, 1):
            for r in range(4):
                arrived(a, 1, slot(1, 1, first, r))
        (forward, backward)[a](256, 256, early, main_tiles, step)

    lane = lax.broadcasted_iota(jnp.int32, (64, 128), 1)
    lane3 = lax.broadcasted_iota(jnp.int32, (4, 16, 128), 2)
    row = lax.broadcasted_iota(jnp.int32, (4, 16, 128), 1)
    for dc in (1, 0):
        for dy in (0, 1):
            for dx in (0, 1):
                at_x = pl.ds((dy * 4 + dc * 2 + dx) * 64, 64)
                at_dy = pl.ds((dx * 4 + dc * 2 + dy) * 64, 64)
                group = dc * 4 + dy * 2 + dx
                at = pl.ds(group * 64, 64)
                info = gx[at_x, pl.ds(width, 128)].astype(jnp.float32).reshape(4, 16, 128)
                info = jnp.sum(jnp.where(row == expert, info, 0.0), axis=1, keepdims=True)
                info = jnp.broadcast_to(info, (4, 16, 128))
                own = (lane3 % 16 == row) & (lane3 < 48)
                weight = jnp.sum(jnp.where(own, info, 0.0), axis=2, keepdims=True).reshape(64, 1)
                pick = jnp.sum(
                    jnp.where(lane3 == 48 + row, info, 0.0), axis=2, keepdims=True
                ).reshape(64, 1)
                pre_gate = pg[at_x, :]
                pre_up = pu[at_x, :]
                back = bg[at_dy, :]
                sig = jax.nn.sigmoid(pre_gate)
                act = pre_gate * sig
                hidden = (act * pre_up).astype(jnp.bfloat16).astype(jnp.float32)
                part_gate = jnp.sum(hidden * back, axis=1, keepdims=True)
                dg[at, :] = (
                    weight * (back * pre_up * sig * (1.0 + pre_gate * (1.0 - sig)))
                ).astype(jnp.bfloat16)
                du[at, :] = (weight * (back * act)).astype(jnp.bfloat16)
                term = jnp.where(
                    (lane + 1).astype(jnp.float32) == pick, jnp.broadcast_to(part_gate, (64, 128)), 0.0
                )
                high = term.astype(jnp.bfloat16)
                low = (term - high.astype(jnp.float32)).astype(jnp.bfloat16)
                blocks = pl.ds(group * 4, 4)
                part[blocks, :, pl.ds(width, 128)] = high.reshape(4, 16, 128)
                part[blocks, :, pl.ds(width + 128, 128)] = low.reshape(4, 16, 128)

    quarter = width // 4
    pieces = [pl.ds(p * quarter, quarter + (256 if p == 3 else 0)) for p in range(4)]

    halves = [
        (
            pl.ds(p * quarter, quarter // 2),
            pl.ds(p * quarter + quarter // 2, quarter // 2 + (256 if p == 3 else 0)),
        )
        for p in range(4)
    ]

    def product(dc, p):
        rows = pl.ds(dc * 256, 256)

        def body(n, carry):
            cols = pl.ds(pl.multiple_of(p * quarter + n * 256, 256), 256)
            out = lax.dot_general(
                dg[rows, :], wg[cols, :], NT, preferred_element_type=jnp.float32
            ) + lax.dot_general(du[rows, :], wu[cols, :], NT, preferred_element_type=jnp.float32)
            part[pl.ds(dc * 16, 16), :, cols] = out.astype(jnp.bfloat16).reshape(16, 16, 256)
            return carry

        lax.fori_loop(0, quarter // 256, body, 0)

    def rs_copy(p, lane_at, src, dst, dev):
        return pltpu.make_async_remote_copy(
            src_ref=src,
            dst_ref=dst,
            send_sem=rs_send.at[p, lane_at],
            recv_sem=rs_recv.at[p, lane_at],
            device_id=dev,
            device_id_type=MESH,
        )

    def add(base, got, got_base, n, cols):
        def body(i, carry):
            total = part[base + i, :, cols].astype(jnp.float32) + got[
                got_base + i, :, cols
            ].astype(jnp.float32)
            part[base + i, :, cols] = total.astype(jnp.bfloat16)
            return carry

        lax.fori_loop(0, n, body, 0)

    flight = {}

    def launch(p, name, *copies):
        for c in copies:
            c.start()
            sends.append((None, c))
        flight[p, name] = copies

    def landed(p, name):
        for c in flight[p, name]:
            c.wait_recv()

    def stage_sib(p):
        cols = pieces[p]
        launch(p, 0, rs_copy(p, 0, part.at[pl.ds(16, 16), :, cols], from_sib.at[:, :, cols], sib))

    def stage_one(p):
        cols = pieces[p]
        landed(p, 0)
        add(0, from_sib, 0, 16, pl.ds(p * quarter, quarter))
        if p == 3:
            hi, lo = pl.ds(width, 128), pl.ds(width + 128, 128)

            def body(i, carry):
                total = (
                    part[i, :, hi].astype(jnp.float32)
                    + part[i, :, lo].astype(jnp.float32)
                    + from_sib[i, :, hi].astype(jnp.float32)
                    + from_sib[i, :, lo].astype(jnp.float32)
                )
                high = total.astype(jnp.bfloat16)
                part[i, :, hi] = high
                part[i, :, lo] = (total - high.astype(jnp.float32)).astype(jnp.bfloat16)
                return carry

            lax.fori_loop(0, 16, body, 0)
        a_cols, b_cols = halves[p]
        launch(
            p,
            1,
            rs_copy(p, 1, part.at[pl.ds(8, 8), :, a_cols], from_one.at[:, :, a_cols], y_nbr),
            rs_copy(p, 2, part.at[pl.ds(4, 4), :, b_cols], from_one.at[pl.ds(0, 4), :, b_cols], x_nbr),
            rs_copy(p, 3, part.at[pl.ds(12, 4), :, b_cols], from_one.at[pl.ds(4, 4), :, b_cols], x_nbr),
        )

    def stage_two(p):
        a_cols, b_cols = halves[p]
        landed(p, 1)
        add(0, from_one, 0, 8, a_cols)
        add(0, from_one, 0, 4, b_cols)
        add(8, from_one, 4, 4, b_cols)
        launch(
            p,
            2,
            rs_copy(p, 4, part.at[pl.ds(4, 4), :, a_cols], from_two.at[:, :, a_cols], x_nbr),
            rs_copy(p, 5, part.at[pl.ds(8, 4), :, b_cols], from_two.at[:, :, b_cols], y_nbr),
        )

    def stage_three(p):
        cols = pieces[p]
        landed(p, 2)
        add(0, from_two, 0, 4, cols)
        launch(
            p,
            3,
            *[
                rs_copy(p, 5 + r, part.at[r, :, cols], from_z.at[r - 1, :, cols], z_peer[r])
                for r in (2, 1, 3)
            ],
        )

    def stage_last(p):
        landed(p, 3)

        def total(cols):
            return (
                part[0, :, cols].astype(jnp.float32)
                + from_z[0, :, cols].astype(jnp.float32)
                + from_z[1, :, cols].astype(jnp.float32)
                + from_z[2, :, cols].astype(jnp.float32)
            )

        cols = pl.ds(p * quarter, quarter)
        dx_out[:, cols] = total(cols).astype(jnp.bfloat16)
        if p == 3:
            gates = total(pl.ds(width, 128)) + total(pl.ds(width + 128, 128))
            gate_out[...] = gates.T[: gate_out.shape[0], :]

    for p in range(4):
        product(1, p)
        stage_sib(p)
        product(0, p)
        stage_one(p)
        if p >= 2:
            stage_two(p - 2)
    stage_three(0)
    stage_two(2)
    stage_three(1)
    stage_two(3)
    stage_three(2)
    stage_last(0)
    stage_three(3)
    for p in (1, 2, 3):
        stage_last(p)
    for cond, c in sends:
        if cond is None:
            c.wait_send()
        else:
            pl.when(cond)(c.wait_send)


def on_device_kernel(tokens, out_grads, routes, gate_values, gate_weight, up_weight, down_weight):
    rows, width = tokens.shape
    experts = lax.axis_size("node") * lax.axis_size("local") // 2
    picks = routes.shape[1]
    expert_ids = jnp.arange(experts, dtype=jnp.int32)[:, None, None]
    hot = routes.T[None, :, :] == expert_ids
    table = jnp.sum(jnp.where(hot, gate_values.T[None, :, :], 0.0), axis=1)
    high = lax.reduce_precision(table, 8, 7)
    mid = lax.reduce_precision(table - high, 8, 7)
    low = table - high - mid
    numbers = jnp.arange(1, picks + 1, dtype=jnp.float32)[None, :, None]
    pick = jnp.sum(jnp.where(hot, numbers, 0.0), axis=1)
    aux = jnp.concatenate([high, mid, low, pick], axis=1)
    aux = jnp.pad(aux, ((0, 0), (0, 128 - 4 * rows))).astype(jnp.bfloat16)
    half = gate_weight.shape[2]
    total = width + 256
    bf16, f32 = jnp.bfloat16, jnp.float32
    dx, gate = pl.pallas_call(
        pair_kernel,
        out_shape=(
            jax.ShapeDtypeStruct((rows, width), bf16),
            jax.ShapeDtypeStruct((picks, rows), f32),
        ),
        in_specs=[pl.BlockSpec(memory_space=pl.ANY)] * 6,
        out_specs=(
            pl.BlockSpec(memory_space=pltpu.VMEM),
            pl.BlockSpec(memory_space=pltpu.VMEM),
        ),
        scratch_shapes=[
            pltpu.VMEM((512, width + 128), bf16),
            pltpu.VMEM((512, width), bf16),
            pltpu.VMEM((width, half), bf16),
            pltpu.VMEM((width, half), bf16),
            pltpu.VMEM((half, width), bf16),
            pltpu.VMEM((512, half), f32),
            pltpu.VMEM((512, half), f32),
            pltpu.VMEM((512, half), f32),
            pltpu.VMEM((512, half), bf16),
            pltpu.VMEM((512, half), bf16),
            pltpu.VMEM((32, 16, total), bf16),
            pltpu.VMEM((16, 16, total), bf16),
            pltpu.VMEM((8, 16, total), bf16),
            pltpu.VMEM((4, 16, total), bf16),
            pltpu.VMEM((3, 16, total), bf16),
            pltpu.SemaphoreType.DMA((6,)),
            pltpu.SemaphoreType.DMA((4, 40)),
            pltpu.SemaphoreType.DMA((4, 32)),
            pltpu.SemaphoreType.DMA((4, 9)),
            pltpu.SemaphoreType.DMA((4, 9)),
        ],
        compiler_params=pltpu.CompilerParams(
            collective_id=0, has_side_effects=True, vmem_limit_bytes=62 * 1024 * 1024
        ),
        cost_estimate=pl.CostEstimate(
            flops=10 * 512 * width * half, bytes_accessed=6 * width * half, transcendentals=0
        ),
    )(tokens, out_grads, aux, gate_weight[0], up_weight[0], down_weight[0])
    return dx, gate.T


def solution(mesh):
    small = mesh.shape["node"] == 8 and mesh.shape["local"] == 4
    in_specs = (
        P(("node", "local"), None),
        P(("node", "local"), None),
        P(("node", "local"), None),
        P(("node", "local"), None),
        P(("node", "local"), None, None),
        P(("node", "local"), None, None),
        P(("node", "local"), None, None),
    )
    out_specs = (P(("node", "local"), None), P(("node", "local"), None))
    body = on_device_kernel if small else on_device
    return jax.shard_map(
        body, mesh=mesh, in_specs=in_specs, out_specs=out_specs, check_vma=False
    )
```

```python
import jax
import jax.numpy as jnp
from jax import lax
from jax.experimental import pallas as pl
from jax.experimental.pallas import tpu as pltpu
from jax.sharding import PartitionSpec as P

NODE_LIMIT = 4
PER_NODE = 2
MESH = pl.DeviceIdType.MESH
NT = (((1,), (1,)), ((), ()))


def shard_terms(rows_x, rows_dy, w_gate, w_up, w_down):
    pre_gate = jnp.dot(rows_x, w_gate, preferred_element_type=jnp.float32)
    pre_up = jnp.dot(rows_x, w_up, preferred_element_type=jnp.float32)
    sigmoid_gate = jax.nn.sigmoid(pre_gate)
    activated = pre_gate * sigmoid_gate
    hidden = (activated * pre_up).astype(jnp.bfloat16)
    back_grad = lax.dot_general(
        rows_dy, w_down, (((1,), (1,)), ((), ())), preferred_element_type=jnp.float32
    )
    part_gate = jnp.sum(hidden.astype(jnp.float32) * back_grad, axis=1)
    d_gate = (back_grad * pre_up * sigmoid_gate * (1.0 + pre_gate * (1.0 - sigmoid_gate))).astype(
        jnp.bfloat16
    )
    d_up = (back_grad * activated).astype(jnp.bfloat16)
    part_dx = lax.dot_general(
        d_gate, w_gate, (((1,), (1,)), ((), ())), preferred_element_type=jnp.float32
    )
    part_dx = part_dx + lax.dot_general(
        d_up, w_up, (((1,), (1,)), ((), ())), preferred_element_type=jnp.float32
    )
    gate_high = part_gate.astype(jnp.bfloat16)
    gate_low = (part_gate - gate_high.astype(jnp.float32)).astype(jnp.bfloat16)
    return (part_dx.astype(jnp.bfloat16), jnp.stack([gate_high, gate_low], axis=-1))


def finish_slots(
    backward_input_gradient, back_gate, position, gate_values, slots, width, row_count, pick_count
):
    flat_index = position.reshape(-1)
    picked = jnp.take(backward_input_gradient.reshape(slots, width), flat_index, axis=0).reshape(
        row_count, pick_count, 2, width
    )
    weighted = jnp.sum(picked.astype(jnp.float32) * gate_values[:, :, None, None], axis=(1, 2))
    gate_parts = jnp.take(back_gate.reshape(slots, 2), flat_index, axis=0).astype(jnp.float32)
    gate_grads = jnp.sum(gate_parts.reshape(row_count, pick_count, 4), axis=2)
    return (weighted.astype(jnp.bfloat16), gate_grads)


def on_device(tokens, out_grads, routes, gate_values, gate_weight, up_weight, down_weight):
    n_node = lax.axis_size("node")
    n_local = lax.axis_size("local")
    devices = n_node * n_local
    row_count = tokens.shape[0]
    pick_count = routes.shape[1]
    width = tokens.shape[1]
    exp_node = n_local // 2
    experts = devices // 2
    node_capacity_limit = min(
        row_count, NODE_LIMIT * (row_count - 1) // (n_node - NODE_LIMIT + 1) + 1
    )
    cap_exp = min(
        node_capacity_limit, PER_NODE * (node_capacity_limit - 1) // (exp_node - PER_NODE + 1) + 1
    )
    w_gate = gate_weight[0]
    w_up = up_weight[0]
    w_down = down_weight[0]
    token_ids = jnp.arange(row_count, dtype=jnp.int32)
    half_ids = jnp.arange(2, dtype=jnp.int32)
    pick_ids = jnp.arange(pick_count, dtype=jnp.int32)
    expert_hot = routes[:, :, None] == jnp.arange(experts, dtype=jnp.int32)[None, None, :]
    per_expert = jnp.any(expert_hot, axis=1).astype(jnp.int32)
    expert_before = jnp.cumsum(per_expert, axis=0) - per_expert
    rank_e = jnp.sum(jnp.where(expert_hot, expert_before[:, None, :], 0), axis=2)
    dest_dev = 2 * routes[:, :, None] + half_ids[None, None, :]
    slots = devices * cap_exp
    node_of = routes // exp_node
    node_hot = node_of[:, :, None] == jnp.arange(n_node, dtype=jnp.int32)[None, None, :]
    per_node = jnp.any(node_hot, axis=1).astype(jnp.int32)
    node_before = jnp.cumsum(per_node, axis=0) - per_node
    node_rank = jnp.sum(jnp.where(node_hot, node_before[:, None, :], 0), axis=2)
    slot_one = (node_of * node_capacity_limit + node_rank).reshape(-1)
    same_before = (node_of[:, :, None] == node_of[:, None, :]) & (
        pick_ids[None, None, :] < pick_ids[None, :, None]
    )
    pick_slot = jnp.sum(same_before.astype(jnp.int32), axis=2).reshape(-1)
    slot_code = (1 + routes % exp_node * cap_exp + rank_e).reshape(-1)
    rows_one = n_node * node_capacity_limit
    owner_ids = jnp.broadcast_to(token_ids[:, None], routes.shape).reshape(-1)
    source_one = (
        jnp.full((rows_one,), row_count, jnp.int32).at[slot_one].set(owner_ids, mode="drop")
    )
    slot_codes = (
        jnp.zeros((rows_one, PER_NODE), jnp.float32)
        .at[slot_one, pick_slot]
        .set(slot_code.astype(jnp.float32), mode="drop")
    )
    slot_codes = slot_codes.astype(jnp.bfloat16).reshape(n_node, node_capacity_limit, PER_NODE)
    send_x = jnp.take(tokens, source_one, axis=0, mode="fill", fill_value=0).reshape(
        n_node, node_capacity_limit, width
    )
    send_dy = jnp.take(out_grads, source_one, axis=0, mode="fill", fill_value=0).reshape(
        n_node, node_capacity_limit, width
    )
    mid_x, mid_dy, mid_payload = (
        lax.all_to_all(send_x, "node", split_axis=0, concat_axis=0, tiled=True),
        lax.all_to_all(send_dy, "node", split_axis=0, concat_axis=0, tiled=True),
        lax.all_to_all(slot_codes, "node", split_axis=0, concat_axis=0, tiled=True),
    )
    mid_payload = mid_payload.reshape(rows_one, -1)
    code_int = mid_payload.astype(jnp.int32)
    is_live = code_int > 0
    local_pick = (code_int - 1) // cap_exp
    slot_rank = (code_int - 1) % cap_exp
    anchor = jnp.arange(rows_one, dtype=jnp.int32) // node_capacity_limit
    dest_two = (
        (2 * local_pick[:, :, None] + half_ids[None, None, :]) * n_node + anchor[:, None, None]
    ) * cap_exp + slot_rank[:, :, None]
    dest_two = jnp.where(is_live[:, :, None], dest_two, slots)
    mid_ids = jnp.broadcast_to(
        jnp.arange(rows_one, dtype=jnp.int32)[:, None, None], dest_two.shape
    ).reshape(-1)
    source_two = (
        jnp.full((slots,), rows_one, jnp.int32).at[dest_two.reshape(-1)].set(mid_ids, mode="drop")
    )
    out_x = jnp.take(mid_x.reshape(rows_one, width), source_two, axis=0, mode="fill", fill_value=0)
    out_dy = jnp.take(
        mid_dy.reshape(rows_one, width), source_two, axis=0, mode="fill", fill_value=0
    )
    got_x, got_dy = (
        lax.all_to_all(
            out_x.reshape(n_local, n_node * cap_exp, width),
            "local",
            split_axis=0,
            concat_axis=0,
            tiled=True,
        ),
        lax.all_to_all(
            out_dy.reshape(n_local, n_node * cap_exp, width),
            "local",
            split_axis=0,
            concat_axis=0,
            tiled=True,
        ),
    )
    part_dx, gate_pair = shard_terms(
        got_x.reshape(slots, width), got_dy.reshape(slots, width), w_gate, w_up, w_down
    )
    backward_input_gradient, back_gate = (
        lax.all_to_all(
            lax.all_to_all(
                part_dx.reshape(n_local, n_node, cap_exp, width),
                "node",
                split_axis=1,
                concat_axis=1,
                tiled=True,
            ),
            "local",
            split_axis=0,
            concat_axis=0,
            tiled=True,
        ),
        lax.all_to_all(
            lax.all_to_all(
                gate_pair.reshape(n_local, n_node, cap_exp, 2),
                "node",
                split_axis=1,
                concat_axis=1,
                tiled=True,
            ),
            "local",
            split_axis=0,
            concat_axis=0,
            tiled=True,
        ),
    )
    position = (dest_dev % n_local * n_node + dest_dev // n_local) * cap_exp + rank_e[:, :, None]
    return finish_slots(
        backward_input_gradient,
        back_gate,
        position,
        gate_values,
        slots,
        width,
        row_count,
        pick_count,
    )


def pair_kernel(
    tok, dyo, aux, wg_hbm, wu_hbm, wd_hbm, dx_out, gate_out,
    gx, gdy, wg, wu, wd, pg, pu, bg, dg, du, part, from_sib, from_one, from_two, from_z,
    local_sem, ag_send, ag_recv, rs_send, rs_recv,
):
    width = tok.shape[1]
    node = lax.axis_index("node")
    local = lax.axis_index("local")
    z, x = node // 2, node % 2
    y, core = local // 2, local % 2
    sib = (node, y * 2 + (1 - core))
    x_nbr = (z * 2 + (1 - x), local)
    y_nbr = (node, (1 - y) * 2 + core)
    z_peer = [None] + [(((z + k) % 4) * 2 + x, local) for k in (1, 2, 3)]
    expert = (node * 4 + local) // 2

    weight_copies = [
        pltpu.make_async_copy(src, dst, local_sem.at[i])
        for i, (src, dst) in enumerate(((wg_hbm, wg), (wu_hbm, wu), (wd_hbm, wd)))
    ]
    own_copies = [
        pltpu.make_async_copy(tok, gx.at[pl.ds(0, 16), pl.ds(0, width)], local_sem.at[3]),
        pltpu.make_async_copy(aux, gx.at[pl.ds(0, 16), pl.ds(width, 128)], local_sem.at[4]),
        pltpu.make_async_copy(dyo, gdy.at[pl.ds(0, 16), :], local_sem.at[5]),
    ]
    for c in own_copies:
        c.start()

    barrier = pltpu.get_barrier_semaphore()
    for dev in [sib, x_nbr, y_nbr] + z_peer[1:]:
        pl.semaphore_signal(barrier, inc=1, device_id=dev, device_id_type=MESH)
    pl.semaphore_wait(barrier, 6)
    for c in own_copies:
        c.wait()

    buffers = (gx, gdy)
    first_nbr = (x_nbr, y_nbr)
    second_nbr = (y_nbr, x_nbr)
    early = 1536
    sends = []
    counts = [0, 0, 0, 0]

    def slot(second, dc, first, r):
        return second * 16 + first * 8 + dc * 4 + r

    def block(a, e, s):
        whole = buffers[a].shape[1]
        cols = pl.ds(0, early) if e == 0 else pl.ds(early, whole - early)
        return buffers[a].at[pl.ds(pl.multiple_of(s * 16, 16), 16), cols]

    def push(a, e, src, dst, dev, cond=None):
        kind = a * 2 + e
        c = pltpu.make_async_remote_copy(
            src_ref=block(a, e, src),
            dst_ref=block(a, e, dst),
            send_sem=ag_send.at[kind, counts[kind]],
            recv_sem=ag_recv.at[kind, dst],
            device_id=dev,
            device_id_type=MESH,
        )
        counts[kind] += 1
        if cond is None:
            c.start()
        else:
            pl.when(cond)(c.start)
        sends.append((cond, c))

    def arrived(a, e, s):
        pltpu.make_async_remote_copy(
            src_ref=block(a, e, s),
            dst_ref=block(a, e, s),
            send_sem=ag_send.at[a * 2 + e, 0],
            recv_sem=ag_recv.at[a * 2 + e, s],
            device_id=sib,
            device_id_type=MESH,
        ).wait_recv()

    def chain_own(a, e, second, first):
        base = slot(second, 0, first, 0)
        push(a, e, base, base + 3, (node + 2, local), z < 3)
        push(a, e, base, base + 1, (node - 2, local), z > 0)

    def chain(a, e, second, first, r):
        base = slot(second, 0, first, 0)
        up = z + r >= 4
        target = jnp.where(up, node + 2, node - 2)
        onward = (up & (z < 3)) | (jnp.logical_not(up) & (z > 0))
        push(a, e, base + r, base + jnp.where(up, r - 1, r + 1), (target, local), onward)

    def to_first(a, e, second, first, r):
        push(a, e, slot(second, 0, first, r), slot(second, 0, 1, r), first_nbr[a])

    def to_second(a, e, second, first, r):
        push(a, e, slot(second, 0, first, r), slot(1, 0, first, r), second_nbr[a])

    def to_sib(a, e, second, first, r):
        push(a, e, slot(second, 0, first, r), slot(second, 1, first, r), sib)

    middle = (z == 1) | (z == 2)
    far = (
        jnp.where(z == 3, 3, 1),
        jnp.where(middle, 3, 2),
        jnp.where(middle, 2, jnp.where(z == 0, 3, 1)),
    )
    both = (0, 1)

    for a in both:
        chain_own(a, 1, 0, 0)
    for a in both:
        to_first(a, 0, 0, 0, 0)
    for a in both:
        to_second(a, 0, 0, 0, 0)
    for a in both:
        to_first(a, 1, 0, 0, 0)
    for a in both:
        to_second(a, 1, 0, 0, 0)
    for a in both:
        chain_own(a, 0, 0, 0)
    for a in both:
        to_sib(a, 1, 0, 0, 0)
        to_sib(a, 0, 0, 0, 0)
    for c in weight_copies:
        c.start()
    for a in both:
        arrived(a, 0, slot(0, 0, 1, 0))
        to_second(a, 0, 0, 1, 0)

    def z_main(j):
        for a in both:
            arrived(a, 1, slot(0, 0, 0, far[j]))
            chain(a, 1, 0, 0, far[j])
            to_first(a, 1, 0, 0, far[j])
            to_second(a, 1, 0, 0, far[j])
            to_sib(a, 1, 0, 0, far[j])

    def first_main(r):
        for a in both:
            arrived(a, 1, slot(0, 0, 1, r))
            to_second(a, 1, 0, 1, r)
            to_sib(a, 1, 0, 1, r)

    def z_early(j):
        for second, first in ((0, 0), (0, 1), (1, 0), (1, 1)):
            for a in both:
                arrived(a, 0, slot(second, 0, first, far[j]))
                chain(a, 0, second, first, far[j])
                to_sib(a, 0, second, first, far[j])

    def second_main(first, r):
        for a in both:
            arrived(a, 1, slot(1, 0, first, r))
            to_sib(a, 1, 1, first, r)

    z_main(0)
    for a in both:
        chain_own(a, 0, 0, 1)
        to_sib(a, 0, 0, 1, 0)
    for first in (0, 1):
        for a in both:
            arrived(a, 0, slot(1, 0, first, 0))
            chain_own(a, 0, 1, first)
            to_sib(a, 0, 1, first, 0)
    z_main(1)
    first_main(0)
    z_main(2)
    z_early(0)
    first_main(far[0])
    z_early(1)
    first_main(far[1])
    first_main(far[2])

    step = (width - early) // 2

    def forward(row, n, start, tiles, width_k):
        rows = pl.ds(row, n)

        def body(k, carry):
            cols = pl.ds(pl.multiple_of(start + k * width_k, 256), width_k)
            left = gx[rows, cols]
            pg[rows, :] += jnp.dot(left, wg[cols, :], preferred_element_type=jnp.float32)
            pu[rows, :] += jnp.dot(left, wu[cols, :], preferred_element_type=jnp.float32)
            return carry

        lax.fori_loop(0, tiles, body, 0)

    def backward(row, n, start, tiles, width_k):
        rows = pl.ds(row, n)

        def body(k, carry):
            cols = pl.ds(pl.multiple_of(start + k * width_k, 256), width_k)
            bg[rows, :] += lax.dot_general(
                gdy[rows, cols], wd[:, cols], NT, preferred_element_type=jnp.float32
            )
            return carry

        lax.fori_loop(0, tiles, body, 0)

    def clear(i, carry):
        rows = pl.ds(pl.multiple_of(i * 64, 64), 64)
        for acc in (pg, pu, bg):
            acc[rows, :] = jnp.zeros((64, 512), jnp.float32)
        return carry

    lax.fori_loop(0, 8, clear, 0)
    for c in weight_copies:
        c.wait()
    main_tiles = (width - early) // step
    for a in both:
        for first in (0, 1):
            for r in range(4):
                arrived(a, 1, slot(0, 1, first, r))
        (forward, backward)[a](0, 256, early, main_tiles, step)
        if a == 0:
            z_early(2)
    def second_products(first):
        for a in both:
            for r in range(4):
                arrived(a, 1, slot(1, 1, first, r))
            (forward, backward)[a](256 + first * 128, 128, early, main_tiles, step)

    for r in (0,) + far:
        second_main(0, r)
    second_products(0)
    second_main(1, 0)
    second_main(1, far[0])
    for a in both:
        for second in (0, 1):
            for first in (0, 1):
                for r in range(4):
                    arrived(a, 0, slot(second, 1, first, r))
        (forward, backward)[a](0, 512, 0, 2, early // 2)
    second_main(1, far[1])
    second_main(1, far[2])
    second_products(1)

    lane = lax.broadcasted_iota(jnp.int32, (64, 128), 1)
    lane3 = lax.broadcasted_iota(jnp.int32, (4, 16, 128), 2)
    row = lax.broadcasted_iota(jnp.int32, (4, 16, 128), 1)
    for dc in (1, 0):
        for dy in (0, 1):
            for dx in (0, 1):
                at_x = pl.ds((dy * 4 + dx * 2 + dc) * 64, 64)
                at_dy = pl.ds((dx * 4 + dy * 2 + dc) * 64, 64)
                group = dc * 4 + dy * 2 + dx
                at = pl.ds(group * 64, 64)
                info = gx[at_x, pl.ds(width, 128)].astype(jnp.float32).reshape(4, 16, 128)
                info = jnp.sum(jnp.where(row == expert, info, 0.0), axis=1, keepdims=True)
                info = jnp.broadcast_to(info, (4, 16, 128))
                own = (lane3 % 16 == row) & (lane3 < 48)
                weight = jnp.sum(jnp.where(own, info, 0.0), axis=2, keepdims=True).reshape(64, 1)
                pick = jnp.sum(
                    jnp.where(lane3 == 48 + row, info, 0.0), axis=2, keepdims=True
                ).reshape(64, 1)
                pre_gate = pg[at_x, :]
                pre_up = pu[at_x, :]
                back = bg[at_dy, :]
                sig = jax.nn.sigmoid(pre_gate)
                act = pre_gate * sig
                hidden = (act * pre_up).astype(jnp.bfloat16).astype(jnp.float32)
                part_gate = jnp.sum(hidden * back, axis=1, keepdims=True)
                dg[at, :] = (
                    weight * (back * pre_up * sig * (1.0 + pre_gate * (1.0 - sig)))
                ).astype(jnp.bfloat16)
                du[at, :] = (weight * (back * act)).astype(jnp.bfloat16)
                term = jnp.where(
                    (lane + 1).astype(jnp.float32) == pick, jnp.broadcast_to(part_gate, (64, 128)), 0.0
                )
                high = term.astype(jnp.bfloat16)
                low = (term - high.astype(jnp.float32)).astype(jnp.bfloat16)
                blocks = pl.ds(group * 4, 4)
                part[blocks, :, pl.ds(width, 128)] = high.reshape(4, 16, 128)
                part[blocks, :, pl.ds(width + 128, 128)] = low.reshape(4, 16, 128)

    sizes = (1024, 1792, 1792, 1536, width - 6144)
    last = len(sizes) - 1
    starts = [sum(sizes[:p]) for p in range(last + 1)]
    tails = [256 if p == last else 0 for p in range(last + 1)]
    pieces = [pl.ds(starts[p], sizes[p] + tails[p]) for p in range(last + 1)]
    halves = [
        (
            pl.ds(starts[p], sizes[p] // 2),
            pl.ds(starts[p] + sizes[p] // 2, sizes[p] // 2 + tails[p]),
        )
        for p in range(last + 1)
    ]

    def product(dc, p):
        rows = pl.ds(dc * 256, 256)

        def body(n, carry):
            cols = pl.ds(pl.multiple_of(starts[p] + n * 256, 256), 256)
            out = lax.dot_general(
                dg[rows, :], wg[cols, :], NT, preferred_element_type=jnp.float32
            ) + lax.dot_general(du[rows, :], wu[cols, :], NT, preferred_element_type=jnp.float32)
            part[pl.ds(dc * 16, 16), :, cols] = out.astype(jnp.bfloat16).reshape(16, 16, 256)
            return carry

        lax.fori_loop(0, sizes[p] // 256, body, 0)

    def rs_copy(p, lane_at, src, dst, dev):
        return pltpu.make_async_remote_copy(
            src_ref=src,
            dst_ref=dst,
            send_sem=rs_send.at[p, lane_at],
            recv_sem=rs_recv.at[p, lane_at],
            device_id=dev,
            device_id_type=MESH,
        )

    def add(base, got, got_base, n, cols):
        def body(i, carry):
            total = part[base + i, :, cols].astype(jnp.float32) + got[
                got_base + i, :, cols
            ].astype(jnp.float32)
            part[base + i, :, cols] = total.astype(jnp.bfloat16)
            return carry

        lax.fori_loop(0, n, body, 0)

    flight = {}

    def launch(p, name, *copies):
        for c in copies:
            c.start()
            sends.append((None, c))
        flight[p, name] = copies

    def landed(p, name):
        for c in flight[p, name]:
            c.wait_recv()

    def stage_sib(p):
        cols = pieces[p]
        launch(p, 0, rs_copy(p, 0, part.at[pl.ds(16, 16), :, cols], from_sib.at[:, :, cols], sib))

    def stage_one(p):
        cols = pieces[p]
        landed(p, 0)
        add(0, from_sib, 0, 16, pl.ds(starts[p], sizes[p]))
        if p == last:
            hi, lo = pl.ds(width, 128), pl.ds(width + 128, 128)

            def body(i, carry):
                total = (
                    part[i, :, hi].astype(jnp.float32)
                    + part[i, :, lo].astype(jnp.float32)
                    + from_sib[i, :, hi].astype(jnp.float32)
                    + from_sib[i, :, lo].astype(jnp.float32)
                )
                high = total.astype(jnp.bfloat16)
                part[i, :, hi] = high
                part[i, :, lo] = (total - high.astype(jnp.float32)).astype(jnp.bfloat16)
                return carry

            lax.fori_loop(0, 16, body, 0)
        a_cols, b_cols = halves[p]
        launch(
            p,
            1,
            rs_copy(p, 1, part.at[pl.ds(8, 8), :, a_cols], from_one.at[:, :, a_cols], y_nbr),
            rs_copy(p, 2, part.at[pl.ds(4, 4), :, b_cols], from_one.at[pl.ds(0, 4), :, b_cols], x_nbr),
            rs_copy(p, 3, part.at[pl.ds(12, 4), :, b_cols], from_one.at[pl.ds(4, 4), :, b_cols], x_nbr),
        )

    def stage_two(p):
        a_cols, b_cols = halves[p]
        landed(p, 1)
        add(0, from_one, 0, 8, a_cols)
        add(0, from_one, 0, 4, b_cols)
        add(8, from_one, 4, 4, b_cols)
        launch(
            p,
            2,
            rs_copy(p, 4, part.at[pl.ds(4, 4), :, a_cols], from_two.at[:, :, a_cols], x_nbr),
            rs_copy(p, 5, part.at[pl.ds(8, 4), :, b_cols], from_two.at[:, :, b_cols], y_nbr),
        )

    def stage_three(p):
        cols = pieces[p]
        landed(p, 2)
        add(0, from_two, 0, 4, cols)
        launch(
            p,
            3,
            *[
                rs_copy(p, 5 + r, part.at[r, :, cols], from_z.at[r - 1, :, cols], z_peer[r])
                for r in (2, 1, 3)
            ],
        )

    def stage_last(p):
        landed(p, 3)

        def total(cols):
            return (
                part[0, :, cols].astype(jnp.float32)
                + from_z[0, :, cols].astype(jnp.float32)
                + from_z[1, :, cols].astype(jnp.float32)
                + from_z[2, :, cols].astype(jnp.float32)
            )

        cols = pl.ds(starts[p], sizes[p])
        dx_out[:, cols] = total(cols).astype(jnp.bfloat16)
        if p == last:
            gates = total(pl.ds(width, 128)) + total(pl.ds(width + 128, 128))
            gate_out[...] = gates.T[: gate_out.shape[0], :]

    for p in range(last + 1):
        product(1, p)
        stage_sib(p)
        product(0, p)
        stage_one(p)
        if p >= 2:
            stage_two(p - 2)
        if p >= 4:
            stage_three(p - 4)
    for p in range(last - 1, last + 1):
        stage_two(p)
        stage_three(p - 2)
        stage_last(p - 3)
    for p in range(last - 1, last + 1):
        stage_three(p)
        stage_last(p - 1)
    stage_last(last)
    for cond, c in sends:
        if cond is None:
            c.wait_send()
        else:
            pl.when(cond)(c.wait_send)


def on_device_kernel(tokens, out_grads, routes, gate_values, gate_weight, up_weight, down_weight):
    rows, width = tokens.shape
    experts = lax.axis_size("node") * lax.axis_size("local") // 2
    picks = routes.shape[1]
    expert_ids = jnp.arange(experts, dtype=jnp.int32)[:, None, None]
    hot = routes.T[None, :, :] == expert_ids
    table = jnp.sum(jnp.where(hot, gate_values.T[None, :, :], 0.0), axis=1)
    high = lax.reduce_precision(table, 8, 7)
    mid = lax.reduce_precision(table - high, 8, 7)
    low = table - high - mid
    numbers = jnp.arange(1, picks + 1, dtype=jnp.float32)[None, :, None]
    pick = jnp.sum(jnp.where(hot, numbers, 0.0), axis=1)
    aux = jnp.concatenate([high, mid, low, pick], axis=1)
    aux = jnp.pad(aux, ((0, 0), (0, 128 - 4 * rows))).astype(jnp.bfloat16)
    half = gate_weight.shape[2]
    total = width + 256
    bf16, f32 = jnp.bfloat16, jnp.float32
    dx, gate = pl.pallas_call(
        pair_kernel,
        out_shape=(
            jax.ShapeDtypeStruct((rows, width), bf16),
            jax.ShapeDtypeStruct((picks, rows), f32),
        ),
        in_specs=[pl.BlockSpec(memory_space=pl.ANY)] * 6,
        out_specs=(
            pl.BlockSpec(memory_space=pltpu.VMEM),
            pl.BlockSpec(memory_space=pltpu.VMEM),
        ),
        scratch_shapes=[
            pltpu.VMEM((512, width + 128), bf16),
            pltpu.VMEM((512, width), bf16),
            pltpu.VMEM((width, half), bf16),
            pltpu.VMEM((width, half), bf16),
            pltpu.VMEM((half, width), bf16),
            pltpu.VMEM((512, half), f32),
            pltpu.VMEM((512, half), f32),
            pltpu.VMEM((512, half), f32),
            pltpu.VMEM((512, half), bf16),
            pltpu.VMEM((512, half), bf16),
            pltpu.VMEM((32, 16, total), bf16),
            pltpu.VMEM((16, 16, total), bf16),
            pltpu.VMEM((8, 16, total), bf16),
            pltpu.VMEM((4, 16, total), bf16),
            pltpu.VMEM((3, 16, total), bf16),
            pltpu.SemaphoreType.DMA((6,)),
            pltpu.SemaphoreType.DMA((4, 40)),
            pltpu.SemaphoreType.DMA((4, 32)),
            pltpu.SemaphoreType.DMA((5, 9)),
            pltpu.SemaphoreType.DMA((5, 9)),
        ],
        compiler_params=pltpu.CompilerParams(
            collective_id=0, has_side_effects=True, vmem_limit_bytes=62 * 1024 * 1024
        ),
        cost_estimate=pl.CostEstimate(
            flops=10 * 512 * width * half, bytes_accessed=6 * width * half, transcendentals=0
        ),
    )(tokens, out_grads, aux, gate_weight[0], up_weight[0], down_weight[0])
    return dx, gate.T


def solution(mesh):
    small = mesh.shape["node"] == 8 and mesh.shape["local"] == 4
    in_specs = (
        P(("node", "local"), None),
        P(("node", "local"), None),
        P(("node", "local"), None),
        P(("node", "local"), None),
        P(("node", "local"), None, None),
        P(("node", "local"), None, None),
        P(("node", "local"), None, None),
    )
    out_specs = (P(("node", "local"), None), P(("node", "local"), None))
    body = on_device_kernel if small else on_device
    return jax.shard_map(
        body, mesh=mesh, in_specs=in_specs, out_specs=out_specs, check_vma=False
    )
```
